256 devices in a mesh: leaf: 32 (over z, x), scene: 8 (over y, core).
Axes of the slice: x: 4, y: 4, z: 8, core: 2. Of those that a mesh axis runs over, the one named last changes fastest.
Arguments:
- features: bfloat16 [8, 256, 8, 8, 8, 128], P('scene', 'leaf'), may hold values from -6 to 6
- weight_first: bfloat16 [27, 128, 128], replicated, may hold values from -0.109375 to 0.109375
- weight_second: bfloat16 [27, 128, 128], replicated, may hold values from -0.109375 to 0.109375
- cotangent: bfloat16 [8, 256, 4, 4, 4, 128], P('scene', 'leaf'), may hold values from -6 to 6
- neighbours: int32 [8, 256, 26], P('scene', 'leaf'), may hold values from -1 to 255, as said below
- voxel_mask: int32 [8, 256, 512], P('scene', 'leaf'), may hold values from 0 to 1, as said below
Outputs:
- coarse: bfloat16 [8, 256, 4, 4, 4, 128], P('scene', 'leaf')
- input_grad: bfloat16 [8, 256, 8, 8, 8, 128], P('scene', 'leaf')
- grad_first: float32 [27, 128, 128], replicated
- grad_second: float32 [27, 128, 128], replicated
The draws below stay inside these ranges and needn't reach their ends.
Inputs may be any that keep to these rules, and one draw needn't show every extreme that they name: `neighbours`: leaf blocks are held 8 to an index of leaf in order. A neighbour found at an offset whose third component is c is held by the index of leaf c away from the leaf's own (the same for c = 0). The relation is symmetric: if n is the neighbour of m at an offset, m is that of n at the opposite offset. An inactive leaf block names no neighbour and is named by none. `voxel_mask`: all voxels of an inactive leaf block are 0; every leaf block of the last index of leaf is active.
All inputs are finite; a program needn't handle non-finite values.
Results may differ from the reference program's by a relative error of at most 0.005.
Values may be sent and summed in bfloat16 or wider, within the bound.
No kernel may reach another device: no remote copies, remote signals or barrier semaphores. Data moves between devices by JAX's collectives and lax.ppermute only.
A program may use at most 128 MiB of HBM per device.

```python
import math
import jax
import jax.numpy as jnp
from jax import lax

C = 128
EDGE = 8
TAPS = 27
LEAF_DEV = 8
HALF = 4
LEAVES = 256
SCENES = 8


offsets = [(a, b, c) for a in (-1, 0, 1) for b in (-1, 0, 1) for c in (-1, 0, 1) if (a, b, c) != (0, 0, 0)]


def leaf_layout(key):
    base = jax.random.fold_in(key, 11)
    key_perm, key_live = jax.random.split(base)
    groups = LEAVES // LEAF_DEV
    cells = 2 * LEAF_DEV
    ranks = jnp.tile(jnp.arange(cells, dtype=jnp.int32), (SCENES * groups, 1))
    order = jax.random.permutation(key_perm, ranks, axis=1, independent=True)
    cell_of = order[:, :LEAF_DEV].reshape(SCENES, LEAVES)
    position = jnp.argsort(order, axis=1, stable=True).astype(jnp.int32)
    occupant = jnp.where(position < LEAF_DEV, position, -1).reshape(SCENES, groups * cells)
    alive = jax.random.randint(key_live, (SCENES, LEAVES), 0, 4) > 0
    final = jnp.arange(LEAVES, dtype=jnp.int32) >= LEAVES - LEAF_DEV
    alive = jnp.logical_or(alive, final[None, :])
    return (cell_of, occupant, alive)


def draw_neighbours(key, part):
    cell_of, occupant, alive = leaf_layout(key)
    groups = LEAVES // LEAF_DEV
    cells = 2 * LEAF_DEV
    holder = jnp.broadcast_to((jnp.arange(LEAVES, dtype=jnp.int32) // LEAF_DEV)[None, :], (SCENES, LEAVES))
    pos_x = cell_of // LEAF_DEV
    pos_y = cell_of % LEAF_DEV
    columns = []
    for a, b, c in offsets:
        target_x = pos_x + a
        target_y = pos_y + b
        target_z = holder + c
        inside = (target_x >= 0) & (target_x < 2) & (target_y >= 0) & (target_y < LEAF_DEV)
        inside = inside & (target_z >= 0) & (target_z < groups)
        clip_x = jnp.clip(target_x, 0, 1)
        clip_y = jnp.clip(target_y, 0, LEAF_DEV - 1)
        clip_z = jnp.clip(target_z, 0, groups - 1)
        where_cell = clip_z * cells + clip_x * LEAF_DEV + clip_y
        target_slot = jnp.take_along_axis(occupant, where_cell, axis=1)
        target = clip_z * LEAF_DEV + jnp.maximum(target_slot, 0)
        target_alive = jnp.take_along_axis(alive, target, axis=1)
        usable = inside & (target_slot >= 0) & target_alive & alive
        columns.append(jnp.where(usable, target, -1))
    return jnp.stack(columns, axis=2).astype(jnp.int32)


def draw_voxel_mask(key, part):
    cell_of, occupant, alive = leaf_layout(key)
    key_vox = jax.random.fold_in(key, 23)
    picks = jax.random.randint(key_vox, (SCENES, LEAVES, EDGE ** 3), 0, 5) < 3
    return jnp.logical_and(picks, alive[:, :, None]).astype(jnp.int32)


def levels(rng, dims, cuts, least, top_value):
    loudness, own = 1.0, jax.random.fold_in(rng, 6)
    for axis_at, shards_of in cuts:
        draws = jnp.exp(jax.random.uniform(jax.random.fold_in(own, axis_at), (shards_of,), jnp.float32, least / len(cuts), top_value / len(cuts)))
        loudness = loudness * jnp.repeat(draws, dims[axis_at] // shards_of).reshape([-1 if axis == axis_at else 1 for axis in range(len(dims))])
    return loudness


def scatter_about(own_key, shape, deviation, limit, shards=(), kind=jnp.bfloat16):
    gain = levels(own_key, shape, shards, -0.22, 0.18) if shards else 1.0
    values = jax.random.normal(own_key, shape, jnp.float32) * deviation * gain
    return jnp.minimum(jnp.maximum(values, -limit), limit).astype(kind)


def setup_inputs(seed: int = 0) -> dict:
    key_list = jax.random.split(jax.random.key(seed), 7)
    features = scatter_about(key_list[0], (SCENES, LEAVES, EDGE, EDGE, EDGE, C), 1.0, 6.0, ((0, 8), (1, 32)))
    weight_first = scatter_about(key_list[1], (TAPS, C, C), (TAPS * C) ** -0.5, 0.109375)
    weight_second = scatter_about(key_list[2], (TAPS, C, C), (TAPS * C) ** -0.5, 0.109375)
    cotangent = scatter_about(key_list[3], (SCENES, LEAVES, HALF, HALF, HALF, C), 1.0, 6.0, ((0, 8), (1, 32)))
    neighbours = draw_neighbours(jax.random.fold_in(key_list[6], 71), 0)
    voxel_mask = draw_voxel_mask(jax.random.fold_in(key_list[6], 71), 0)
    return {"features": features, "weight_first": weight_first, "weight_second": weight_second, "cotangent": cotangent, "neighbours": neighbours, "voxel_mask": voxel_mask}


offsets = [(a, b, c) for a in (-1, 0, 1) for b in (-1, 0, 1) for c in (-1, 0, 1) if (a, b, c) != (0, 0, 0)]

def pad_range(shift, edge_len):
    if shift < 0:
        return slice(0, 1)
    if shift > 0:
        return slice(edge_len + 1, edge_len + 2)
    return slice(1, edge_len + 1)

def leaf_range(shift, edge_len):
    if shift < 0:
        return slice(edge_len - 1, edge_len)
    if shift > 0:
        return slice(0, 1)
    return slice(0, edge_len)

def assemble(interior, source, lookup, usable):
    edge_len = interior.shape[1]
    padded = jnp.pad(interior, ((0, 0), (1, 1), (1, 1), (1, 1), (0, 0)))
    for direction, (a, b, c) in enumerate(offsets):
        slab_part = source[:, leaf_range(a, edge_len), leaf_range(b, edge_len), leaf_range(c, edge_len), :]
        picked = jnp.take(slab_part, lookup[:, direction], axis=0)
        keep = usable[:, direction][:, None, None, None, None]
        picked = jnp.where(keep, picked, jnp.zeros_like(picked))
        padded = padded.at[:, pad_range(a, edge_len), pad_range(b, edge_len), pad_range(c, edge_len), :].set(picked)
    return padded

def conv_forward(padded, weight, stride):
    leaves = padded.shape[0]
    edge_len = padded.shape[1] - 2
    out_edge = edge_len // stride
    channels = weight.shape[2]
    summed = jnp.zeros((leaves * out_edge ** 3, channels), jnp.float32)
    for tap_id in range(weight.shape[0]):
        p, q, r = (tap_id // 9, tap_id // 3 % 3, tap_id % 3)
        window = padded[:, p:p + edge_len:stride, q:q + edge_len:stride, r:r + edge_len:stride, :]
        summed = summed + jnp.dot(window.reshape(-1, window.shape[-1]), weight[tap_id], preferred_element_type=jnp.float32)
    return summed.reshape(leaves, out_edge, out_edge, out_edge, channels)

def weight_grad(padded, upstream, stride):
    edge_len = padded.shape[1] - 2
    flat_up = upstream.reshape(-1, upstream.shape[-1])
    parts = []
    for tap_id in range(27):
        p, q, r = (tap_id // 9, tap_id // 3 % 3, tap_id % 3)
        window = padded[:, p:p + edge_len:stride, q:q + edge_len:stride, r:r + edge_len:stride, :]
        parts.append(jnp.dot(window.reshape(-1, window.shape[-1]).T, flat_up, preferred_element_type=jnp.float32))
    return jnp.stack(parts)

def conv_adjoint(upstream, weight, stride, edge_len):
    leaves = upstream.shape[0]
    out_edge = upstream.shape[1]
    channels = weight.shape[1]
    back_pad = jnp.zeros((leaves, edge_len + 2, edge_len + 2, edge_len + 2, channels), jnp.float32)
    flat_up = upstream.reshape(-1, upstream.shape[-1])
    for tap_id in range(weight.shape[0]):
        p, q, r = (tap_id // 9, tap_id // 3 % 3, tap_id % 3)
        term = jnp.dot(flat_up, weight[tap_id].T, preferred_element_type=jnp.float32)
        term = term.reshape(leaves, out_edge, out_edge, out_edge, channels)
        back_pad = back_pad.at[:, p:p + edge_len:stride, q:q + edge_len:stride, r:r + edge_len:stride, :].add(term)
    return back_pad

def route_back(back_pad, lookup, usable, row_total):
    edge_len = back_pad.shape[1] - 2
    channels = back_pad.shape[-1]
    target = jnp.zeros((row_total, edge_len, edge_len, edge_len, channels), jnp.float32)
    for direction, (a, b, c) in enumerate(offsets):
        slab_part = back_pad[:, pad_range(a, edge_len), pad_range(b, edge_len), pad_range(c, edge_len), :]
        keep = usable[:, direction][:, None, None, None, None]
        slab_part = jnp.where(keep, slab_part, jnp.zeros_like(slab_part))
        target = target.at[lookup[:, direction], leaf_range(a, edge_len), leaf_range(b, edge_len), leaf_range(c, edge_len), :].add(slab_part)
    return target

def reference(features, weight_first, weight_second, cotangent, neighbours, voxel_mask):

    def one_scene(inputs):
        scene_feat, scene_cot, scene_nbr, scene_mask = inputs
        leaves = scene_feat.shape[0]
        edge_len = scene_feat.shape[1]
        mask_f = scene_mask.reshape(leaves, edge_len, edge_len, edge_len, 1).astype(jnp.float32)
        masked = scene_feat * mask_f.astype(jnp.bfloat16)
        usable = scene_nbr >= 0
        lookup = jnp.clip(scene_nbr, 0, leaves - 1).astype(jnp.int32)
        padded_in = assemble(masked, masked, lookup, usable)
        pre_act = conv_forward(padded_in, weight_first, 1)
        sigma = jax.nn.sigmoid(pre_act)
        hidden = (mask_f * pre_act * sigma).astype(jnp.bfloat16)
        padded_hidden = assemble(hidden, hidden, lookup, usable)
        coarse_mask = mask_f[:, ::2, ::2, ::2]
        coarse = (coarse_mask * conv_forward(padded_hidden, weight_second, 2)).astype(jnp.bfloat16)
        coarse_grad = scene_cot * coarse_mask.astype(jnp.bfloat16)
        grad_second = weight_grad(padded_hidden, coarse_grad, 2)
        back_second = conv_adjoint(coarse_grad, weight_second, 2, edge_len)
        inner = slice(1, edge_len + 1)
        grad_hidden = back_second[:, inner, inner, inner, :] + route_back(back_second, lookup, usable, leaves)
        slope = sigma * (1.0 + pre_act * (1.0 - sigma))
        delta = (grad_hidden * mask_f * slope).astype(jnp.bfloat16)
        grad_first = weight_grad(padded_in, delta, 1)
        back_first = conv_adjoint(delta, weight_first, 1, edge_len)
        input_grad = back_first[:, inner, inner, inner, :] + route_back(back_first, lookup, usable, leaves)
        input_grad = (input_grad * mask_f).astype(jnp.bfloat16)
        return (coarse, input_grad, grad_first, grad_second)
    coarse, input_grad, grad_first, grad_second = lax.map(one_scene, (features, cotangent, neighbours, voxel_mask))
    factor = 1.0 / math.sqrt(SCENES * LEAVES * EDGE ** 3)
    return (coarse, input_grad, lax.optimization_barrier(jnp.sum(grad_first, axis=0)) * factor, lax.optimization_barrier(jnp.sum(grad_second, axis=0)) * factor)
```

```python
import math

import jax
import jax.numpy as jnp
from jax import lax
from jax.experimental import pallas as pl
from jax.experimental.pallas import tpu as pltpu
from jax.sharding import PartitionSpec as P

bf16 = jnp.bfloat16
f32 = jnp.float32
C = 128
L = 8
E = 8
ROWS = 64
SPAN = 9 * C
PARAMS = pltpu.CompilerParams(vmem_limit_bytes=58 * 1024 * 1024)


def place(table, leaf, a, b, c):
    return table[leaf, 9 * (a + 1) + 3 * (b + 1) + (c + 1)]


def edge_row(face, block, i, j):
    return jnp.broadcast_to(face[block, i, pl.ds(j, 1), :], (E, C))


def columns(table, lines, low, high, leaf, x, top):
    first, last = x == 0, x == top + 1
    a = jnp.where(first, -1, jnp.where(last, 1, 0))
    i = jnp.where(first, top - 1, jnp.where(last, 0, x - 1))
    ids = lax.broadcasted_iota(jnp.int32, (E, C), 0)
    out = ([], [], [])
    for y in range(E + 2):
        b = -1 if y == 0 else 1 if y == E + 1 else 0
        j = E - 1 if y == 0 else 0 if y == E + 1 else y - 1
        line = lines[place(table, leaf, a, b, 0), i, j]
        below = pltpu.roll(line, 1, 0)
        above = pltpu.roll(line, E - 1, 0)
        if low is not None:
            below = jnp.where(ids == 0, edge_row(low, place(table, leaf, a, b, -1), i, j), below)
        else:
            below = jnp.where(ids == 0, 0.0, below)
        above = jnp.where(ids == E - 1, edge_row(high, place(table, leaf, a, b, 1), i, j), above)
        for r, part in enumerate((below, line, above)):
            out[r].append(part)
    return [jnp.concatenate(part, axis=0) for part in out]


def fill_columns(table, lines, low, high, leaf, x, top, store):
    cols = columns(table, lines, low, high, leaf, x, top)
    for q in range(3):
        for r in range(3):
            store((3 * q + r) * C, cols[r][E * q : E * q + ROWS].astype(bf16))


def banded(weight, first, second, shift):
    zero = jnp.zeros((SPAN, C), bf16)
    w = [weight[9 * s : 9 * s + 9].reshape(SPAN, C) for s in range(3)]
    first[:SPAN, :C] = w[0]
    first[:SPAN, C:] = zero
    first[SPAN:, :C] = w[1]
    first[SPAN:, C:] = w[0]
    second[:SPAN, :C] = w[2]
    second[:SPAN, C:] = w[1]
    second[SPAN:, :C] = zero
    second[SPAN:, C:] = w[2]


def pairs_dot(cols, leaf, first, second):
    lo = cols[leaf, 0:4].reshape(4 * ROWS, 2 * SPAN)
    hi = cols[leaf, 1:5].reshape(4 * ROWS, 2 * SPAN)
    return jnp.dot(lo, first[...], preferred_element_type=f32) + jnp.dot(hi, second[...], preferred_element_type=f32)


def first_kernel(
    table, feat, mask, low_in, high_in, cot, cot_high_in, w1, w2t,
    hidden, delta, grad,
    lines, low, high, clines, chigh, cols, ccols, wa, wb, turned, total,
):
    lines[L] = jnp.zeros((E, E, E, C), f32)
    low[L] = jnp.zeros((E, E, C), f32)
    high[L] = jnp.zeros((E, E, C), f32)
    clines[L] = jnp.zeros((4, E, E, C), f32)
    chigh[L] = jnp.zeros((4, E, C), f32)

    @pl.loop(0, L)
    def _(leaf):
        lines[leaf] = feat[leaf].astype(f32) * mask[leaf].astype(f32)
        low[leaf] = low_in[leaf].astype(f32)
        high[leaf] = high_in[leaf].astype(f32)
        clines[leaf] = cot[leaf].astype(f32)
        chigh[leaf] = cot_high_in[leaf].astype(f32)

    banded(w1, wa, wb, 0)

    @pl.loop(0, L)
    def _(leaf):
        @pl.loop(0, 5)
        def _(pair):
            for half in range(2):
                def store(at, value, half=half):
                    cols[leaf, pair, :, pl.ds(half * SPAN + at, C)] = value
                fill_columns(table, lines, low, high, leaf, 2 * pair + half, E, store)

            def store_c(at, value):
                ccols[pair, :, pl.ds(at, C)] = value
            fill_columns(table, clines, None, chigh, leaf, pair + 1, 4, store_c)

        pre = pairs_dot(cols, leaf, wa, wb)
        g = jnp.dot(ccols[0:4].reshape(4 * ROWS, SPAN), w2t[:, 0 : 2 * C], preferred_element_type=f32)
        g1 = jnp.dot(ccols[1:5].reshape(4 * ROWS, SPAN), w2t[:, 2 * C :], preferred_element_type=f32)
        sig = 1.0 / (1.0 + jnp.exp(-pre))
        slope = sig * (1.0 + pre * (1.0 - sig))
        for half in range(2):
            at = slice(half * C, half * C + C)
            m = mask[leaf].reshape(4, 2, ROWS, C)[:, half].reshape(4 * ROWS, C).astype(f32)
            h = (m * pre[:, at] * sig[:, at]).astype(bf16)
            gg = g[:, at] if half == 0 else g[:, at] + g1
            d = (gg * m * slope[:, at]).astype(bf16)
            hidden[leaf, :, half] = h.reshape(4, ROWS, C)
            delta[leaf, :, half] = d.reshape(4, ROWS, C)
            turned[half * C : half * C + C, pl.ds(pl.multiple_of(leaf * 256, 256), 256)] = d.T

    total[...] = jnp.zeros_like(total)
    for tile in range(9):
        at = slice(256 * tile, 256 * tile + 256)
        for step in range(2):
            rhs = cols[:, step : step + 4, :, at].reshape(L * 4 * ROWS, 256)
            for half in range(2):
                res = None
                for side in range(2):
                    p = 2 * step + side - half
                    lanes = [lane for lane in range(256 * tile, 256 * tile + 256, C) if lane // SPAN == side]
                    if not 0 <= p <= 2 or not lanes:
                        continue
                    if res is None:
                        res = jnp.dot(turned[half * C : half * C + C, :], rhs, preferred_element_type=f32)
                    for lane in lanes:
                        o = lane - SPAN * side
                        total[p, :, o : o + C] += res[:, lane - 256 * tile : lane - 256 * tile + C]
    for p in range(3):
        for t in range(9):
            grad[9 * p + t] = total[p, :, t * C : t * C + C].T.astype(grad.dtype)


def smem():
    return pl.BlockSpec(memory_space=pltpu.SMEM)


def vmem():
    return pl.BlockSpec(memory_space=pltpu.VMEM)


def first_call(table, feat, mask, low, high, cot, cot_high, w1, w2t, gdt=bf16):
    return pl.pallas_call(
        first_kernel,
        out_shape=(
            jax.ShapeDtypeStruct((L, 4, 2, ROWS, C), bf16),
            jax.ShapeDtypeStruct((L, 4, 2, ROWS, C), bf16),
            jax.ShapeDtypeStruct((27, C, C), gdt),
        ),
        in_specs=[smem()] + [vmem()] * 8,
        out_specs=(vmem(), vmem(), vmem()),
        scratch_shapes=[
            pltpu.VMEM((L + 1, E, E, E, C), f32),
            pltpu.VMEM((L + 1, E, E, C), f32),
            pltpu.VMEM((L + 1, E, E, C), f32),
            pltpu.VMEM((L + 1, 4, E, E, C), f32),
            pltpu.VMEM((L + 1, 4, E, C), f32),
            pltpu.VMEM((L, 5, ROWS, 2 * SPAN), bf16),
            pltpu.VMEM((5, ROWS, SPAN), bf16),
            pltpu.VMEM((2 * SPAN, 2 * C), bf16),
            pltpu.VMEM((2 * SPAN, 2 * C), bf16),
            pltpu.VMEM((2 * C, L * 256), bf16),
            pltpu.VMEM((3, C, SPAN), f32),
        ],
        compiler_params=PARAMS,
        cost_estimate=pl.CostEstimate(flops=8_000_000_000, bytes_accessed=8_000_000, transcendentals=0),
        name="first_conv",
    )(table, feat, mask, low, high, cot, cot_high, w1, w2t)


def adjoint_kernel(table, delta, mask, low_in, high_in, w, out, lines, low, high, cols, wa, wb):
    lines[L] = jnp.zeros((E, E, E, C), f32)
    low[L] = jnp.zeros((E, E, C), f32)
    high[L] = jnp.zeros((E, E, C), f32)

    @pl.loop(0, L)
    def _(leaf):
        lines[leaf] = delta[leaf].astype(f32)
        low[leaf] = low_in[leaf].astype(f32)
        high[leaf] = high_in[leaf].astype(f32)

    banded(w, wa, wb, 0)

    @pl.loop(0, L)
    def _(leaf):
        @pl.loop(0, 5)
        def _(pair):
            for half in range(2):
                def store(at, value, half=half):
                    cols[leaf % 2, pair, :, pl.ds(half * SPAN + at, C)] = value
                fill_columns(table, lines, low, high, leaf, 2 * pair + half, E, store)
        res = pairs_dot(cols, leaf % 2, wa, wb)
        for half in range(2):
            at = slice(half * C, half * C + C)
            m = mask[leaf].reshape(4, 2, ROWS, C)[:, half].reshape(4 * ROWS, C).astype(f32)
            out[leaf, :, half] = (res[:, at] * m).astype(bf16).reshape(4, ROWS, C)


def adjoint_call(table, delta, mask, low, high, w):
    return pl.pallas_call(
        adjoint_kernel,
        out_shape=jax.ShapeDtypeStruct((L, 4, 2, ROWS, C), bf16),
        in_specs=[smem()] + [vmem()] * 5,
        out_specs=vmem(),
        scratch_shapes=[
            pltpu.VMEM((L + 1, E, E, E, C), f32),
            pltpu.VMEM((L + 1, E, E, C), f32),
            pltpu.VMEM((L + 1, E, E, C), f32),
            pltpu.VMEM((2, 5, ROWS, 2 * SPAN), bf16),
            pltpu.VMEM((2 * SPAN, 2 * C), bf16),
            pltpu.VMEM((2 * SPAN, 2 * C), bf16),
        ],
        compiler_params=PARAMS,
        cost_estimate=pl.CostEstimate(flops=4_000_000_000, bytes_accessed=5_000_000, transcendentals=0),
        name="first_adjoint",
    )(table, delta, mask, low, high, w)


def second_kernel(table, hidden, low_in, cot, cmask, w2, coarse, grad, lines, low, cols, turned, total):
    lines[L] = jnp.zeros((E, E, E, C), f32)
    low[L] = jnp.zeros((E, E, C), f32)

    @pl.loop(0, L)
    def _(leaf):
        lines[leaf] = hidden[leaf].astype(f32)
        low[leaf] = low_in[leaf].astype(f32)

    ids = lax.broadcasted_iota(jnp.int32, (E, C), 0)
    w = w2[...].reshape(27 * C, C)

    @pl.loop(0, L)
    def _(leaf):
        @pl.loop(0, 5)
        def _(pair):
            for half in range(2):
                x = 2 * pair + half
                first = x == 0
                a = jnp.where(first, -1, 0)
                i = jnp.where(first, E - 1, jnp.minimum(x - 1, E - 1))
                out = ([], [], [])
                for y in range(E + 1):
                    b = -1 if y == 0 else 0
                    j = E - 1 if y == 0 else y - 1
                    line = lines[place(table, leaf, a, b, 0), i, j]
                    below = jnp.where(ids == 0, edge_row(low, place(table, leaf, a, b, -1), i, j), pltpu.roll(line, 1, 0))
                    above = pltpu.roll(line, E - 1, 0)
                    for r, part in enumerate((below, line, above)):
                        out[r].append(part)
                for q in range(3):
                    for r in range(3):
                        value = jnp.concatenate([out[r][q + 2 * m] for m in range(4)], axis=0).astype(bf16)
                        cols[leaf, pair, :, pl.ds(half * SPAN + (3 * q + r) * C, C)] = value
        lo = cols[leaf, 0:4].reshape(128, 2 * SPAN)
        hi = cols[leaf, 1:5, :, 0:SPAN].reshape(128, SPAN)
        res = jnp.dot(lo, w[: 2 * SPAN], preferred_element_type=f32) + jnp.dot(hi, w[2 * SPAN :], preferred_element_type=f32)
        coarse[leaf] = (res.reshape(4, 4, E, C) * cmask[leaf].astype(f32)).astype(bf16)
        d = cot[leaf].reshape(128, C)
        turned[:, pl.ds(pl.multiple_of(leaf * 128, 128), 128)] = d.T

    for tile in range(9):
        at = slice(256 * tile, 256 * tile + 256)
        rhs = cols[:, 0:4, :, at].reshape(L * 128, 256)
        total[:, at] = jnp.dot(turned[...], rhs, preferred_element_type=f32)
    for tile in range(5):
        hi = min(256 * tile + 256, SPAN)
        rhs = cols[:, 1:5, :, 256 * tile : hi].reshape(L * 128, hi - 256 * tile)
        total[:, 2 * SPAN + 256 * tile : 2 * SPAN + hi] = jnp.dot(turned[...], rhs, preferred_element_type=f32)
    for t in range(27):
        grad[t] = total[:, t * C : t * C + C].T.astype(grad.dtype)


def second_call(table, hidden, low, cot, cmask, w2, gdt=bf16):
    return pl.pallas_call(
        second_kernel,
        out_shape=(
            jax.ShapeDtypeStruct((L, 4, 4, E, C), bf16),
            jax.ShapeDtypeStruct((27, C, C), gdt),
        ),
        in_specs=[smem()] + [vmem()] * 5,
        out_specs=(vmem(), vmem()),
        scratch_shapes=[
            pltpu.VMEM((L + 1, E, E, E, C), f32),
            pltpu.VMEM((L + 1, E, E, C), f32),
            pltpu.VMEM((L, 5, 32, 2 * SPAN), bf16),
            pltpu.VMEM((C, L * 128), bf16),
            pltpu.VMEM((C, 3 * SPAN), f32),
        ],
        compiler_params=PARAMS,
        cost_estimate=pl.CostEstimate(flops=2_000_000_000, bytes_accessed=5_000_000, transcendentals=0),
        name="second_conv",
    )(table, hidden, low, cot, cmask, w2)


def passed(block, distance):
    count = lax.axis_size("leaf")
    return lax.ppermute(block, "leaf", [(i - distance, i) for i in range(count) if 0 <= i - distance < count])


def local_table(neighbours):
    found = jnp.where(neighbours >= 0, neighbours % L, L)
    own = jnp.arange(L, dtype=jnp.int32)[:, None]
    return jnp.concatenate([found[:, :13], own, found[:, 13:]], axis=1)


def spread(x, dims):
    cfg = [(0, 1, 1) if d in dims else (0, 0, 0) for d in range(x.ndim)]
    return lax.pad(x, jnp.zeros((), x.dtype), cfg)


def pieces_summed(pieces):
    return jnp.sum(pieces.astype(f32), axis=0)


def summed_everywhere(first, second):
    scene_count, leaf_count = lax.axis_size("scene"), lax.axis_size("leaf")
    core = lax.axis_index("scene") % 2
    swap = [(i, i ^ 1) for i in range(scene_count)]
    ring = [[c + 2 * y for y in range(scene_count // 2)] for c in range(2)]
    quarters = scene_count // 2
    rows = C // 2 // quarters
    taps = 2 * 27
    per = -(-taps // leaf_count)
    both = jnp.concatenate([first, second], axis=0).reshape(taps, 2, C // 2, C)
    kept = lax.dynamic_index_in_dim(both, core, axis=1, keepdims=False)
    sent = lax.dynamic_index_in_dim(both, 1 - core, axis=1, keepdims=False)
    with jax.named_scope("sum_core"):
        half = kept.astype(f32) + lax.ppermute(sent.astype(bf16), "scene", swap).astype(f32)
    with jax.named_scope("sum_y"):
        parts = half.reshape(taps, quarters, rows, C).swapaxes(0, 1).astype(bf16)
        quarter = pieces_summed(lax.all_to_all(parts, "scene", 0, 0, axis_index_groups=ring, tiled=True).reshape(quarters, taps, rows, C))
    with jax.named_scope("sum_leaf"):
        parts = jnp.pad(quarter.astype(bf16), ((0, per * leaf_count - taps), (0, 0), (0, 0))).reshape(leaf_count, per * rows, C)
        own = pieces_summed(lax.all_to_all(parts, "leaf", 0, 0, tiled=True))
    factor = 1.0 / math.sqrt(leaf_count * scene_count * L * E**3)
    own = (own * factor).astype(bf16)
    with jax.named_scope("gather_leaf"):
        parts = jnp.broadcast_to(own[None], (leaf_count, per * rows, C))
        quarter = lax.all_to_all(parts, "leaf", 0, 0, tiled=True).reshape(per * leaf_count, rows, C)[:taps]
    with jax.named_scope("gather_y"):
        parts = jnp.broadcast_to(quarter[None], (quarters, taps, rows, C))
        half = lax.all_to_all(parts, "scene", 0, 0, axis_index_groups=ring, tiled=True)
    with jax.named_scope("gather_core"):
        other = lax.ppermute(half, "scene", swap)
    low = jnp.where(core == 0, half, other)
    high = jnp.where(core == 0, other, half)
    whole = jnp.stack([low, high], axis=0).reshape(2, quarters, taps, rows, C)
    whole = whole.transpose(2, 0, 1, 3, 4).reshape(taps, C, C).astype(f32)
    return whole[:27], whole[27:]


def shards(features, weight_first, weight_second, cotangent, neighbours, voxel_mask):
    feat = features[0]
    cot = cotangent[0]
    voxels = voxel_mask[0].reshape(L, E, E, E, 1).astype(bf16)
    mask = jnp.broadcast_to(voxels, (L, E, E, E, C))
    table = local_table(neighbours[0])
    coarse_mask = voxels[:, ::2, ::2, ::2]
    coarse_grad = cot * coarse_mask
    up = feat[:, :, :, E - 1] * voxels[:, :, :, E - 1]
    down = feat[:, :, :, 0] * voxels[:, :, :, 0]
    with jax.named_scope("faces_in"):
        low = passed(up, 1)
        down = jnp.concatenate([down.reshape(L, ROWS, C), coarse_grad[:, :, :, 0].reshape(L, 16, C)], axis=1)
        high = passed(down, -1)
    cot_high = spread(high[:, ROWS:].reshape(L, 4, 4, C), (2,))
    high = high[:, :ROWS].reshape(L, E, E, C)
    turned_first = jnp.swapaxes(weight_first[::-1], 1, 2)
    turned_second = jnp.swapaxes(weight_second[::-1], 1, 2).reshape(3, SPAN, C)
    turned_second = jnp.concatenate([turned_second[1], turned_second[0], turned_second[2]], axis=1)
    hidden, delta, grad_first = first_call(
        table, feat, mask, low, high, spread(coarse_grad, (2, 3)), cot_high, weight_first, turned_second
    )
    hidden = hidden.reshape(L, E, E, E, C)
    delta = delta.reshape(L, E, E, E, C)
    with jax.named_scope("faces_mid"):
        tops = jnp.stack([hidden[:, :, :, E - 1], delta[:, :, :, E - 1]], axis=0)
        tops = passed(tops, 1)
        bottom = passed(delta[:, :, :, 0], -1)
    coarse, grad_second = second_call(
        table, hidden, tops[0], spread(coarse_grad, (3,)),
        spread(jnp.broadcast_to(coarse_mask, (L, 4, 4, 4, C)), (3,)), weight_second
    )
    coarse = coarse[:, :, :, ::2]
    grad_first, grad_second = summed_everywhere(grad_first, grad_second)
    input_grad = adjoint_call(table, delta, mask, tops[1], bottom, turned_first).reshape(L, E, E, E, C)
    return (coarse[None], input_grad[None], grad_first, grad_second)


def solution(mesh):
    placed = (
        P("scene", "leaf", None, None, None, None),
        P(),
        P(),
        P("scene", "leaf", None, None, None, None),
        P("scene", "leaf", None),
        P("scene", "leaf", None),
    )
    return jax.shard_map(
        shards,
        mesh=mesh,
        in_specs=placed,
        out_specs=(
            P("scene", "leaf", None, None, None, None),
            P("scene", "leaf", None, None, None, None),
            P(),
            P(),
        ),
        check_vma=False,
    )
```

```python
import math

import jax
import jax.numpy as jnp
from jax import lax
from jax.experimental import pallas as pl
from jax.experimental.pallas import tpu as pltpu
from jax.sharding import PartitionSpec as P

bf16 = jnp.bfloat16
f32 = jnp.float32
C = 128
L = 8
E = 8
FACE = E * E
SPAN = 9 * C
TAPS = 27
HALF = C // 2
PIECE = 16


def smem():
    return pl.BlockSpec(memory_space=pltpu.SMEM)


def vmem():
    return pl.BlockSpec(memory_space=pltpu.VMEM)


def params(mebibytes):
    return pltpu.CompilerParams(vmem_limit_bytes=mebibytes * 1024 * 1024)


def cost(flops, size):
    return pl.CostEstimate(flops=int(flops), bytes_accessed=int(size), transcendentals=0)


def edge_row(face, block, i, j):
    return jnp.broadcast_to(face[block, i, pl.ds(j, 1), :], (E, C))


def source_plane(x, top):
    if isinstance(x, int):
        a = 0 if x == 0 else 18 if x == top + 1 else 9
        return a, top - 1 if x == 0 else 0 if x == top + 1 else x - 1
    first, last = x == 0, x == top + 1
    return jnp.where(first, 0, jnp.where(last, 18, 9)), jnp.where(first, top - 1, jnp.where(last, 0, x - 1))


def shifted_lines(table, lines, low, high, leaf, x, top, rows):
    a, i = source_plane(x, top)
    at = [[table[leaf, a + 3 * b + c] for c in range(3)] for b in range(3)]
    ids = lax.broadcasted_iota(jnp.int32, (E, C), 0)
    out = ([], [], [])
    for y in rows:
        b = 0 if y == 0 else 2 if y == E + 1 else 1
        j = E - 1 if y == 0 else 0 if y == E + 1 else y - 1
        line = lines[at[b][1], i, E * j : E * j + E]
        below = jnp.where(ids == 0, 0.0 if low is None else edge_row(low, at[b][0], i, j), pltpu.roll(line, 1, 0))
        above = pltpu.roll(line, E - 1, 0)
        if high is not None:
            above = jnp.where(ids == E - 1, edge_row(high, at[b][2], i, j), above)
        for r, part in enumerate((below, line, above)):
            out[r].append(part)
    return out


def fill_plane(store, *where):
    parts = shifted_lines(*where, range(E + 2))
    whole = [jnp.concatenate(part, axis=0) for part in parts]
    for q in range(3):
        for r in range(3):
            store((3 * q + r) * C, whole[r][E * q : E * q + FACE].astype(bf16))


def banded(weight, first, second):
    zero = jnp.zeros((SPAN, C), bf16)
    w = [weight[9 * s : 9 * s + 9].reshape(SPAN, C) for s in range(3)]
    first[:SPAN, :C] = w[0]
    first[:SPAN, C:] = zero
    first[SPAN:, :C] = w[1]
    first[SPAN:, C:] = w[0]
    second[:SPAN, :C] = w[2]
    second[:SPAN, C:] = w[1]
    second[SPAN:, :C] = zero
    second[SPAN:, C:] = w[2]


def banded_turned(weight, first, second):
    zero = jnp.zeros((C, SPAN), bf16)
    w = [jnp.concatenate([weight[TAPS - 1 - t] for t in range(9 * s, 9 * s + 9)], axis=1) for s in range(3)]
    first[:C, :SPAN] = w[0]
    first[C:, :SPAN] = zero
    first[:C, SPAN:] = w[1]
    first[C:, SPAN:] = w[0]
    second[:C, :SPAN] = w[2]
    second[C:, :SPAN] = w[1]
    second[:C, SPAN:] = zero
    second[C:, SPAN:] = w[2]


def dot(x, w):
    return jnp.dot(x, w, preferred_element_type=f32)


def dot_turned(x, w):
    return lax.dot_general(x, w, (((1,), (1,)), ((), ())), preferred_element_type=f32)


def pairs_dot(multiply, cols, at, first, second):
    lo = cols[at, 0:4].reshape(4 * FACE, 2 * SPAN)
    hi = cols[at, 1:5].reshape(4 * FACE, 2 * SPAN)
    return multiply(lo, first[...]) + multiply(hi, second[...])


def half_planes(ref, leaf, half):
    return jnp.concatenate([ref[leaf, 2 * pair + half] for pair in range(4)], axis=0)


def prepare_kernel(voxels, feat, cot, mask, up, down, spread, held, coarse):
    @pl.loop(0, L)
    def _(leaf):
        row = jnp.broadcast_to(voxels[pl.ds(leaf, 1), :].astype(f32), (C, E**3))
        whole = row.T
        spread[...] = whole
        mask[leaf] = whole.reshape(E, FACE, C).astype(bf16)
        held[...] = feat[leaf].reshape(E**3, C).astype(f32) * whole
        up[leaf] = held[pl.ds(E - 1, FACE, stride=E), :].astype(bf16)
        down[leaf, 0:FACE] = held[pl.ds(0, FACE, stride=E), :].astype(bf16)
        coarse[...] = cot[leaf].astype(f32)
        edge = coarse[pl.ds(0, 16, stride=4), :]
        active = jnp.concatenate([spread[pl.ds(2 * FACE * i, 4, stride=16), :] for i in range(4)], axis=0)
        down[leaf, FACE : FACE + 16] = (edge * active).astype(bf16)


def prepare(voxels, feat, cot):
    return pl.pallas_call(
        prepare_kernel,
        out_shape=(
            jax.ShapeDtypeStruct((L, E, FACE, C), bf16),
            jax.ShapeDtypeStruct((L, FACE, C), bf16),
            jax.ShapeDtypeStruct((L, FACE + 16, C), bf16),
        ),
        in_specs=[vmem()] * 3,
        out_specs=(vmem(),) * 3,
        scratch_shapes=[pltpu.VMEM((E**3, C), f32), pltpu.VMEM((E**3, C), f32), pltpu.VMEM((64, C), f32)],
        compiler_params=params(16),
        name="prepare",
    )(voxels, feat, cot)


def first_kernel(
    table, feat, mask, low_in, high_in, cot, w1, w2,
    cols, hidden, delta, up, down,
    lines, low, high, clines, chigh, ccols, coarse, wa, wb, wc, faces,
):
    step = pl.program_id(0)

    @pl.when(step == 0)
    def _():
        lines[L] = jnp.zeros((E, FACE, C), f32)
        low[L] = jnp.zeros((E, E, C), f32)
        high[L] = jnp.zeros((E, E, C), f32)
        clines[L] = jnp.zeros((4, FACE, C), f32)
        chigh[...] = jnp.zeros((L + 1, 4, E, C), f32)

        @pl.loop(0, L)
        def _(leaf):
            lines[leaf] = feat[leaf].astype(f32) * mask[leaf].astype(f32)
            low[leaf] = low_in[leaf].astype(f32).reshape(E, E, C)
            high[leaf] = high_in[leaf, 0:FACE].astype(f32).reshape(E, E, C)
            coarse[0:16] = high_in[leaf, FACE : FACE + 16].astype(f32)
            for i in range(4):
                chigh[leaf, i, pl.ds(0, 4, stride=2), :] = coarse[4 * i : 4 * i + 4]
            coarse[...] = cot[leaf].astype(f32)
            clines[leaf] = jnp.zeros((4, FACE, C), f32)
            for i in range(4):
                for j in range(4):
                    clines[leaf, i, pl.ds(16 * j, 4, stride=2), :] = coarse[16 * i + 4 * j : 16 * i + 4 * j + 4]
                clines[leaf, i] = clines[leaf, i] * mask[leaf, 2 * i].astype(f32)

        banded(w1, wa, wb)
        for n, p in enumerate((1, 2, 0)):
            for t in range(9):
                wc[n * C : n * C + C, t * C : t * C + C] = w2[9 * p + 8 - t]

    for pair in range(5):
        for half in range(2):
            def store(at, value, pair=pair, half=half):
                cols[0, pair, :, half * SPAN + at : half * SPAN + at + C] = value
            fill_plane(store, table, lines, low, high, step, 2 * pair + half, E)

        def store_coarse(at, value, pair=pair):
            ccols[pair, :, at : at + C] = value
        fill_plane(store_coarse, table, clines, None, chigh, step, pair + 1, 4)

    pre = pairs_dot(dot, cols, 0, wa, wb)
    back = dot_turned(ccols[0:4].reshape(4 * FACE, SPAN), wc[: 2 * C])
    back_next = dot_turned(ccols[1:5].reshape(4 * FACE, SPAN), wc[2 * C :])
    sig = 1.0 / (1.0 + jnp.exp(-pre))
    slope = sig * (1.0 + pre * (1.0 - sig))
    for half in range(2):
        at = slice(half * C, half * C + C)
        m = half_planes(mask, step, half).astype(f32)
        h = m * pre[:, at] * sig[:, at]
        g = back[:, at] if half == 0 else back[:, at] + back_next
        d = g * m * slope[:, at]
        for pair in range(4):
            rows = slice(FACE * pair, FACE * pair + FACE)
            hidden[0, 2 * pair + half] = h[rows].astype(bf16)
            delta[0, 2 * pair + half] = d[rows].astype(bf16)
            faces[0, 2 * pair + half] = h[rows]
            faces[1, 2 * pair + half] = d[rows]
    for i in range(0, E, 2):
        def face(which, k, i=i):
            return jnp.concatenate([faces[which, i + n, pl.ds(k, E, stride=E), :] for n in range(2)], axis=0).astype(bf16)
        rows = slice(E * i, E * i + 2 * E)
        up[0, 0, rows] = face(0, E - 1)
        up[1, 0, rows] = face(1, E - 1)
        down[0, rows] = face(1, 0)


def first_conv(table, feat, mask, low, high, cot, w1, w2):
    def leafwise(*shape):
        return pl.BlockSpec((1, *shape), lambda s: (s,) + (0,) * len(shape))

    return pl.pallas_call(
        first_kernel,
        grid=(L,),
        out_shape=(
            jax.ShapeDtypeStruct((L, 5, FACE, 2 * SPAN), bf16),
            jax.ShapeDtypeStruct((L, E, FACE, C), bf16),
            jax.ShapeDtypeStruct((L, E, FACE, C), bf16),
            jax.ShapeDtypeStruct((2, L, FACE, C), bf16),
            jax.ShapeDtypeStruct((L, FACE, C), bf16),
        ),
        in_specs=[smem()] + [vmem()] * 7,
        out_specs=(
            leafwise(5, FACE, 2 * SPAN),
            leafwise(E, FACE, C),
            leafwise(E, FACE, C),
            pl.BlockSpec((2, 1, FACE, C), lambda s: (0, s, 0, 0)),
            leafwise(FACE, C),
        ),
        scratch_shapes=[
            pltpu.VMEM((L + 1, E, FACE, C), f32),
            pltpu.VMEM((L + 1, E, E, C), f32),
            pltpu.VMEM((L + 1, E, E, C), f32),
            pltpu.VMEM((L + 1, 4, FACE, C), f32),
            pltpu.VMEM((L + 1, 4, E, C), f32),
            pltpu.VMEM((5, FACE, SPAN), bf16),
            pltpu.VMEM((64, C), f32),
            pltpu.VMEM((2 * SPAN, 2 * C), bf16),
            pltpu.VMEM((2 * SPAN, 2 * C), bf16),
            pltpu.VMEM((3 * C, SPAN), bf16),
            pltpu.VMEM((2, E, FACE, C), f32),
        ],
        compiler_params=params(28),
        cost_estimate=cost(15e9, 18e6),
        name="first_conv",
    )(table, feat, mask, low, high, cot, w1, w2)


def split_halves(core, whole, kept, sent):
    mine = pl.multiple_of(core * HALF, HALF)
    theirs = pl.multiple_of(HALF - core * HALF, HALF)
    for t in range(TAPS):
        kept[t] = whole[t, pl.ds(mine, HALF), :]
        sent[t] = whole[t, pl.ds(theirs, HALF), :].astype(bf16)


def first_grad_kernel(core, cols, delta, kept, sent, turned, total, whole):
    @pl.loop(0, L)
    def _(leaf):
        for half in range(2):
            turned[half * C : half * C + C, pl.ds(pl.multiple_of(leaf * 256, 256), 256)] = half_planes(delta, leaf, half).T

    total[...] = jnp.zeros_like(total)
    for tile in range(9):
        lanes = range(256 * tile, 256 * tile + 256, C)
        for next_pair in range(2):
            rhs = cols[:, next_pair : next_pair + 4, :, 256 * tile : 256 * tile + 256].reshape(L * 4 * FACE, 256)
            for half in range(2):
                use = [lane for lane in lanes if 0 <= 2 * next_pair + lane // SPAN - half <= 2]
                if not use:
                    continue
                res = dot(turned[half * C : half * C + C, :], rhs)
                for lane in use:
                    p, o = 2 * next_pair + lane // SPAN - half, lane % SPAN
                    total[p, :, o : o + C] += res[:, lane - 256 * tile : lane - 256 * tile + C]

    for p in range(3):
        for t in range(9):
            whole[9 * p + t] = total[p, :, t * C : t * C + C].T
    split_halves(core[0], whole, kept, sent)


def halves_shape():
    return jax.ShapeDtypeStruct((TAPS, HALF, C), f32), jax.ShapeDtypeStruct((TAPS, HALF, C), bf16)


def first_grad(core, cols, delta):
    return pl.pallas_call(
        first_grad_kernel,
        out_shape=halves_shape(),
        in_specs=[smem(), vmem(), vmem()],
        out_specs=(vmem(), vmem()),
        scratch_shapes=[
            pltpu.VMEM((2 * C, L * 256), bf16),
            pltpu.VMEM((3, C, SPAN), f32),
            pltpu.VMEM((TAPS, C, C), f32),
        ],
        compiler_params=params(16),
        cost_estimate=cost(6e9, 14e6),
        name="first_grad",
    )(core, cols, delta)


def second_kernel(
    table, core, hidden, low_in, cot, mask, w2,
    coarse, kept, sent,
    lines, low, cols, turned, total, whole, thin,
):
    lines[L] = jnp.zeros((E, FACE, C), f32)
    low[L] = jnp.zeros((E, E, C), f32)
    thin[0] = jnp.zeros((2 * FACE, C), f32)

    @pl.loop(0, L)
    def _(leaf):
        lines[leaf] = hidden[leaf].astype(f32)
        low[leaf] = low_in[leaf].astype(f32).reshape(E, E, C)

    w = w2[...].reshape(TAPS * C, C)

    @pl.loop(0, L)
    def _(leaf):
        for x in range(E + 1):
            parts = shifted_lines(table, lines, low, None, leaf, x, E, range(E + 1))
            for q in range(3):
                for r in range(3):
                    value = jnp.concatenate([parts[r][q + 2 * m] for m in range(4)], axis=0).astype(bf16)
                    at = (x % 2) * SPAN + (3 * q + r) * C
                    cols[leaf, x // 2, :, at : at + C] = value
        lo = cols[leaf, 0:4].reshape(2 * FACE, 2 * SPAN)
        hi = cols[leaf, 1:5, :, 0:SPAN].reshape(2 * FACE, SPAN)
        res = jnp.dot(lo, w[: 2 * SPAN], preferred_element_type=f32) + jnp.dot(hi, w[2 * SPAN :], preferred_element_type=f32)
        active = []
        for i in range(4):
            plane = mask[leaf, 2 * i].astype(f32)
            active += [plane[16 * j : 16 * j + E] for j in range(4)]
        active = jnp.concatenate(active, axis=0)
        thin[1] = res * active
        coarse[leaf] = thin[1, pl.ds(0, FACE, stride=2), :].astype(bf16)
        thin[0, pl.ds(0, FACE, stride=2), :] = cot[leaf].astype(f32)
        upstream = (thin[0] * active).astype(bf16)
        turned[:, pl.ds(pl.multiple_of(leaf * 128, 128), 128)] = upstream.T

    for tile in range(9):
        at = slice(256 * tile, 256 * tile + 256)
        total[:, at] = jnp.dot(turned[...], cols[:, 0:4, :, at].reshape(L * 2 * FACE, 256), preferred_element_type=f32)
    for tile in range(5):
        end = min(256 * tile + 256, SPAN)
        rhs = cols[:, 1:5, :, 256 * tile : end].reshape(L * 2 * FACE, end - 256 * tile)
        total[:, 2 * SPAN + 256 * tile : 2 * SPAN + end] = jnp.dot(turned[...], rhs, preferred_element_type=f32)
    for t in range(TAPS):
        whole[t] = total[:, t * C : t * C + C].T
    split_halves(core[0], whole, kept, sent)


def second_conv(table, core, hidden, low, cot, mask, w2):
    return pl.pallas_call(
        second_kernel,
        out_shape=(jax.ShapeDtypeStruct((L, 64, C), bf16), *halves_shape()),
        in_specs=[smem()] * 2 + [vmem()] * 5,
        out_specs=(vmem(),) * 3,
        scratch_shapes=[
            pltpu.VMEM((L + 1, E, FACE, C), f32),
            pltpu.VMEM((L + 1, E, E, C), f32),
            pltpu.VMEM((L, 5, 32, 2 * SPAN), bf16),
            pltpu.VMEM((C, L * 128), bf16),
            pltpu.VMEM((C, 3 * SPAN), f32),
            pltpu.VMEM((TAPS, C, C), f32),
            pltpu.VMEM((2, 2 * FACE, C), f32),
        ],
        compiler_params=params(40),
        cost_estimate=cost(8e9, 6e6),
        name="second_conv",
    )(table, core, hidden, low, cot, mask, w2)


def adjoint_kernel(start, count, table, delta, mask, low_in, high_in, w, out, lines, low, high, cols, wa, wb):
    lines[L] = jnp.zeros((E, FACE, C), f32)
    low[L] = jnp.zeros((E, E, C), f32)
    high[L] = jnp.zeros((E, E, C), f32)

    @pl.loop(0, L)
    def _(leaf):
        lines[leaf] = delta[leaf].astype(f32)
        low[leaf] = low_in[leaf].astype(f32).reshape(E, E, C)
        high[leaf] = high_in[leaf].astype(f32).reshape(E, E, C)

    banded_turned(w, wa, wb)

    @pl.loop(0, count)
    def _(n):
        for pair in range(5):
            for half in range(2):
                def store(at, value, pair=pair, half=half):
                    cols[0, pair, :, half * SPAN + at : half * SPAN + at + C] = value
                fill_plane(store, table, lines, low, high, start + n, 2 * pair + half, E)
        res = pairs_dot(dot_turned, cols, 0, wa, wb)
        for half in range(2):
            m = half_planes(mask, start + n, half).astype(f32)
            value = (res[:, half * C : half * C + C] * m).astype(bf16)
            for pair in range(4):
                out[n, 2 * pair + half] = value[FACE * pair : FACE * pair + FACE]


def adjoint_conv(start, count, table, delta, mask, low, high, w):
    def kernel(*refs):
        adjoint_kernel(start, count, *refs)

    return pl.pallas_call(
        kernel,
        out_shape=jax.ShapeDtypeStruct((count, E, FACE, C), bf16),
        in_specs=[smem()] + [vmem()] * 5,
        out_specs=vmem(),
        scratch_shapes=[
            pltpu.VMEM((L + 1, E, FACE, C), f32),
            pltpu.VMEM((L + 1, E, E, C), f32),
            pltpu.VMEM((L + 1, E, E, C), f32),
            pltpu.VMEM((1, 5, FACE, 2 * SPAN), bf16),
            pltpu.VMEM((2 * C, 2 * SPAN), bf16),
            pltpu.VMEM((2 * C, 2 * SPAN), bf16),
        ],
        compiler_params=params(32),
        cost_estimate=cost(10e9 * count / L, 6e6),
        name="first_adjoint",
    )(table, delta, mask, low, high, w)


def start_sum_kernel(place, kept1, got1, kept2, got2, own, *sends):
    mine = place[0]
    for d in range(4):
        rows = pl.ds(pl.multiple_of(((mine + d) % 4) * PIECE, PIECE), PIECE)
        for t in range(2 * TAPS):
            kept, got, n = (kept1, got1, t) if t < TAPS else (kept2, got2, t - TAPS)
            value = kept[n, rows, :] + got[n, rows, :].astype(f32)
            if d == 0:
                own[t] = value
            else:
                sends[d - 1][t] = value.astype(bf16)


def start_sum(place, kept1, got1, kept2, got2):
    return pl.pallas_call(
        start_sum_kernel,
        out_shape=(jax.ShapeDtypeStruct((2 * TAPS, PIECE, C), f32),) + (jax.ShapeDtypeStruct((2 * TAPS, PIECE, C), bf16),) * 3,
        in_specs=[smem()] + [vmem()] * 4,
        out_specs=(vmem(),) * 4,
        compiler_params=params(12),
        cost_estimate=cost(1e6, 3e6),
        name="start_sum",
    )(place, kept1, got1, kept2, got2)


def next_sum_kernel(own, a, b, c, out):
    value = own[...] + a[...].astype(f32) + b[...].astype(f32) + c[...].astype(f32)
    out[0 : 2 * TAPS] = value.astype(bf16)
    out[2 * TAPS :] = jnp.zeros((out.shape[0] - 2 * TAPS, PIECE, C), bf16)


def next_sum(own, received, taps):
    return pl.pallas_call(
        next_sum_kernel,
        out_shape=jax.ShapeDtypeStruct((taps, PIECE, C), bf16),
        in_specs=[vmem()] * 4,
        out_specs=vmem(),
        compiler_params=params(8),
        cost_estimate=cost(1e6, 2e6),
        name="next_sum",
    )(own, *received)


def last_sum_kernel(factor, parts, out):
    total = parts[0].astype(f32)
    for n in range(1, parts.shape[0]):
        total = total + parts[n].astype(f32)
    total = (total * factor).astype(bf16)
    for n in range(parts.shape[0]):
        out[n] = total


def last_sum(parts, factor):
    def kernel(*refs):
        last_sum_kernel(factor, *refs)

    return pl.pallas_call(
        kernel,
        out_shape=jax.ShapeDtypeStruct(parts.shape, bf16),
        in_specs=[vmem()],
        out_specs=vmem(),
        compiler_params=params(8),
        cost_estimate=cost(1e6, 1e6),
        name="last_sum",
    )(parts)


def finish_kernel(place, *refs):
    mine, theirs, (first, second) = refs[0:4], refs[4:8], refs[8:10]

    for d in range(4):
        for parts, core, at in ((mine, place[2], place[0]), (theirs, 1 - place[2], place[1])):
            row = pl.multiple_of(core * HALF + ((at - d + 4) % 4) * PIECE, PIECE)
            for t in range(2 * TAPS):
                out, n = (first, t) if t < TAPS else (second, t - TAPS)
                out[n, pl.ds(row, PIECE), :] = parts[d][t].astype(f32)


def finish(place, pieces):
    return pl.pallas_call(
        finish_kernel,
        out_shape=(jax.ShapeDtypeStruct((TAPS, C, C), f32),) * 2,
        in_specs=[smem()] + [vmem()] * 8,
        out_specs=(vmem(),) * 2,
        compiler_params=params(12),
        cost_estimate=cost(1e6, 6e6),
        name="finish",
    )(place, *pieces)


def ring_orders(leaf_count):
    out = []
    for d in range(1, 4):
        pairs = []
        for leaf in range(leaf_count):
            for scene in range(8):
                z, x, y, core = leaf // 4, leaf % 4, scene // 2, scene % 2
                x, y = (x, (y + d) % 4) if core == 0 else ((x + d) % 4, y)
                pairs.append((leaf * 8 + scene, (z * 4 + x) * 8 + y * 2 + core))
        out.append(pairs)
    return out


def rest_groups(leaf_count):
    depth = leaf_count // 4
    first = [[(z * 4 + x) * 8 + 2 * y for z in range(depth) for x in range(4)] for y in range(4)]
    second = [[(z * 4 + x) * 8 + 2 * y + 1 for z in range(depth) for y in range(4)] for x in range(4)]
    return first + second


def passed(block, distance):
    count = lax.axis_size("leaf")
    return lax.ppermute(block, "leaf", [(i - distance, i) for i in range(count) if 0 <= i - distance < count])


def to_other_core(block):
    return lax.ppermute(block, "scene", [(i, i ^ 1) for i in range(lax.axis_size("scene"))])


def local_table(neighbours):
    found = jnp.where(neighbours >= 0, neighbours % L, L)
    own = jnp.arange(L, dtype=jnp.int32)[:, None]
    return jnp.concatenate([found[:, :13], own, found[:, 13:]], axis=1)


def shards(features, weight_first, weight_second, cotangent, neighbours, voxel_mask):
    both = ("leaf", "scene")
    leaf_count, scene_count = lax.axis_size("leaf"), lax.axis_size("scene")
    leaf_at, scene_at = lax.axis_index("leaf"), lax.axis_index("scene")
    core, x_at, y_at = scene_at % 2, leaf_at % 4, scene_at // 2
    place = jnp.stack([jnp.where(core == 0, y_at, x_at), jnp.where(core == 0, x_at, y_at), core]).astype(jnp.int32)
    core = place[2:3]
    feat = features[0].reshape(L, E, FACE, C)
    cot = cotangent[0].reshape(L, 64, C)
    table = local_table(neighbours[0])

    mask, up, down = prepare(voxel_mask[0], feat, cot)
    with jax.named_scope("faces_in"):
        low = passed(up, 1)
        high = passed(down, -1)
    cols, hidden, delta, up, down = first_conv(table, feat, mask, low, high, cot, weight_first, weight_second)
    with jax.named_scope("faces_mid"):
        tops = passed(up, 1)
        bottom = passed(down, -1)
    kept1, sent1 = first_grad(core, cols, delta)
    with jax.named_scope("sum_core"):
        got1 = to_other_core(sent1)
    coarse, kept2, sent2 = second_conv(table, core, hidden, tops[0], cot, mask, weight_second)
    with jax.named_scope("sum_core"):
        got2 = to_other_core(sent2)
    own, *sends = start_sum(place, kept1, got1, kept2, got2)
    orders, groups = ring_orders(leaf_count), rest_groups(leaf_count)
    per = -(-2 * TAPS // leaf_count)
    with jax.named_scope("sum_ring"):
        received = [lax.ppermute(s, both, o) for s, o in zip(sends, orders)]
    input_grad = adjoint_conv(0, L, table, delta, mask, tops[1], bottom, weight_first)
    own, input_grad = lax.optimization_barrier((own, input_grad))
    parts = next_sum(own, received, per * leaf_count).reshape(leaf_count, per * PIECE, C)
    with jax.named_scope("sum_rest"):
        parts = lax.all_to_all(parts, both, 0, 0, axis_index_groups=groups, tiled=True)
    parts = last_sum(parts, 1.0 / math.sqrt(leaf_count * scene_count * L * E**3))
    with jax.named_scope("gather_rest"):
        parts = lax.all_to_all(parts, both, 0, 0, axis_index_groups=groups, tiled=True)
    own = parts.reshape(per * leaf_count, PIECE, C)[: 2 * TAPS]
    with jax.named_scope("gather_ring"):
        mine = [own] + [lax.ppermute(own, both, o) for o in orders]
    with jax.named_scope("gather_core"):
        theirs = [to_other_core(piece) for piece in mine]
    grad_first, grad_second = finish(place, mine + theirs)
    return (
        coarse.reshape(1, L, 4, 4, 4, C),
        input_grad.reshape(1, L, E, E, E, C),
        grad_first,
        grad_second,
    )


def solution(mesh):
    placed = (
        P("scene", "leaf", None, None, None, None),
        P(),
        P(),
        P("scene", "leaf", None, None, None, None),
        P("scene", "leaf", None),
        P("scene", "leaf", None),
    )
    return jax.shard_map(
        shards,
        mesh=mesh,
        in_specs=placed,
        out_specs=(
            P("scene", "leaf", None, None, None, None),
            P("scene", "leaf", None, None, None, None),
            P(),
            P(),
        ),
        check_vma=False,
    )
```

```python
import math

import jax
import jax.numpy as jnp
from jax import lax
from jax.experimental import pallas as pl
from jax.experimental.pallas import tpu as pltpu
from jax.sharding import PartitionSpec as P

bf16 = jnp.bfloat16
f32 = jnp.float32
C = 128
L = 8
E = 8
FACE = E * E
SPAN = 9 * C
TAPS = 27
HALF = C // 2
PER = 2
PIECE = 16


def core_at():
    return lax.axis_index("scene") & 1


def ring_at():
    return jnp.where(core_at() == 0, lax.axis_index("scene") >> 1, lax.axis_index("leaf") & 3)


def smem():
    return pl.BlockSpec(memory_space=pltpu.SMEM)


def vmem():
    return pl.BlockSpec(memory_space=pltpu.VMEM)


def params(mebibytes):
    return pltpu.CompilerParams(vmem_limit_bytes=mebibytes * 1024 * 1024)


def cost(flops, size):
    return pl.CostEstimate(flops=int(flops), bytes_accessed=int(size), transcendentals=0)


def edge_row(face, block, i, j):
    return jnp.broadcast_to(face[block, i, pl.ds(j, 1), :], (E, C))


def source_plane(x, top):
    return -1 if x == 0 else 1 if x == top + 1 else 0, top - 1 if x == 0 else 0 if x == top + 1 else x - 1


def block_at(neighbours, leaf, a, b, c):
    d = 9 * a + 3 * b + c
    if d == 0:
        return leaf
    n = neighbours[leaf, 13 + d if d < 0 else 12 + d]
    return jnp.where(n < 0, L, n & (L - 1))


def shifted_lines(table, lines, low, high, leaf, x, top, rows):
    a, i = source_plane(x, top)
    ends = (-1, 0, 1)
    at = [[block_at(table, leaf, a, b, c) if (c < 0 and low is not None) or c == 0 or (c > 0 and high is not None) else None for c in ends] for b in ends]
    ids = lax.broadcasted_iota(jnp.int32, (E, C), 0)
    out = ([], [], [])
    for y in rows:
        b = 0 if y == 0 else 2 if y == E + 1 else 1
        j = E - 1 if y == 0 else 0 if y == E + 1 else y - 1
        line = lines[at[b][1], i, E * j : E * j + E]
        below = jnp.where(ids == 0, 0.0 if low is None else edge_row(low, at[b][0], i, j), pltpu.roll(line, 1, 0))
        above = pltpu.roll(line, E - 1, 0)
        if high is not None:
            above = jnp.where(ids == E - 1, edge_row(high, at[b][2], i, j), above)
        for r, part in enumerate((below, line, above)):
            out[r].append(part)
    return out


def fill_plane(store, *where):
    parts = shifted_lines(*where, range(E + 2))
    whole = [jnp.concatenate(part, axis=0) for part in parts]
    for q in range(3):
        for r in range(3):
            store((3 * q + r) * C, whole[r][E * q : E * q + FACE].astype(bf16))


def banded(weight, first, second):
    zero = jnp.zeros((SPAN, C), bf16)
    w = [weight[9 * s : 9 * s + 9].reshape(SPAN, C) for s in range(3)]
    first[:SPAN, :C] = w[0]
    first[:SPAN, C:] = zero
    first[SPAN:, :C] = w[1]
    first[SPAN:, C:] = w[0]
    second[:SPAN, :C] = w[2]
    second[:SPAN, C:] = w[1]
    second[SPAN:, :C] = zero
    second[SPAN:, C:] = w[2]


def banded_turned(weight, first, second):
    zero = jnp.zeros((C, SPAN), bf16)
    w = [jnp.concatenate([weight[TAPS - 1 - t] for t in range(9 * s, 9 * s + 9)], axis=1) for s in range(3)]
    first[:C, :SPAN] = w[0]
    first[C:, :SPAN] = zero
    first[:C, SPAN:] = w[1]
    first[C:, SPAN:] = w[0]
    second[:C, :SPAN] = w[2]
    second[C:, :SPAN] = w[1]
    second[:C, SPAN:] = zero
    second[C:, SPAN:] = w[2]


def dot(x, w):
    return jnp.dot(x, w, preferred_element_type=f32)


def dot_turned(x, w):
    return lax.dot_general(x, w, (((1,), (1,)), ((), ())), preferred_element_type=f32)


def pairs_dot(multiply, cols, at, first, second):
    lo = cols[at, 0:4].reshape(4 * FACE, 2 * SPAN)
    hi = cols[at, 1:5].reshape(4 * FACE, 2 * SPAN)
    return multiply(lo, first[...]) + multiply(hi, second[...])


def half_planes(ref, leaf, half):
    return jnp.concatenate([ref[leaf, 2 * pair + half] for pair in range(4)], axis=0)


def spread_mask(voxels, leaf):
    return jnp.broadcast_to(voxels[leaf : leaf + 1, :].astype(f32), (C, E**3)).T


def faces_kernel(voxels, feat, cot, up, down, spread, held, coarse):
    for leaf in range(L):
        whole = spread_mask(voxels, leaf)
        spread[...] = whole
        coarse[...] = cot[leaf].astype(f32)
        edge = coarse[pl.ds(0, 16, stride=4), :]
        active = jnp.concatenate([spread[pl.ds(2 * FACE * i, 4, stride=16), :] for i in range(4)], axis=0)
        down[leaf, FACE : FACE + 16] = (edge * active).astype(bf16)
        held[...] = feat[leaf].reshape(E**3, C).astype(f32) * whole
        up[leaf] = held[pl.ds(E - 1, FACE, stride=E), :].astype(bf16)
        down[leaf, 0:FACE] = held[pl.ds(0, FACE, stride=E), :].astype(bf16)


def first_faces(voxels, feat, cot):
    return pl.pallas_call(
        faces_kernel,
        out_shape=(
            jax.ShapeDtypeStruct((L, FACE, C), bf16),
            jax.ShapeDtypeStruct((L, FACE + 16, C), bf16),
        ),
        in_specs=[vmem()] * 3,
        out_specs=(vmem(),) * 2,
        scratch_shapes=[pltpu.VMEM((E**3, C), f32), pltpu.VMEM((E**3, C), f32), pltpu.VMEM((64, C), f32)],
        compiler_params=params(12),
        cost_estimate=cost(6e9, 8e6),
        name="first_faces",
    )(voxels, feat, cot)


def setup_kernel(voxels, feat, cot, w1, w2, mask, lines, clines, wa, wb, wc, spread, coarse):
    lines[L] = jnp.zeros((E, FACE, C), f32)
    clines[...] = jnp.zeros((L + 1, 4, FACE, C), f32)
    for leaf in range(L):
        whole = spread_mask(voxels, leaf)
        spread[...] = whole
        mask[leaf] = whole.reshape(E, FACE, C).astype(bf16)
        lines[leaf] = feat[leaf].astype(f32) * whole.reshape(E, FACE, C)
        coarse[...] = cot[leaf].astype(f32)
        for i in range(4):
            for j in range(4):
                clines[leaf, i, pl.ds(16 * j, 4, stride=2), :] = coarse[16 * i + 4 * j : 16 * i + 4 * j + 4]
            clines[leaf, i] = clines[leaf, i] * spread[2 * FACE * i : 2 * FACE * i + FACE]
    banded(w1, wa, wb)
    for n, p in enumerate((1, 2, 0)):
        for t in range(9):
            wc[n * C : n * C + C, t * C : t * C + C] = w2[9 * p + 8 - t]


def setup(voxels, feat, cot, w1, w2):
    return pl.pallas_call(
        setup_kernel,
        out_shape=(
            jax.ShapeDtypeStruct((L, E, FACE, C), bf16),
            jax.ShapeDtypeStruct((L + 1, E, FACE, C), f32),
            jax.ShapeDtypeStruct((L + 1, 4, FACE, C), f32),
            jax.ShapeDtypeStruct((2 * SPAN, 2 * C), bf16),
            jax.ShapeDtypeStruct((2 * SPAN, 2 * C), bf16),
            jax.ShapeDtypeStruct((3 * C, SPAN), bf16),
        ),
        in_specs=[vmem()] * 5,
        out_specs=(vmem(),) * 6,
        scratch_shapes=[pltpu.VMEM((E**3, C), f32), pltpu.VMEM((64, C), f32)],
        compiler_params=params(14),
        cost_estimate=cost(1e9, 8e6),
        name="setup",
    )(voxels, feat, cot, w1, w2)


def first_kernel(
    table, lines, clines, mask, low_in, high_in, wa, wb, wc,
    cols, hidden, delta, up, down,
    low, high, chigh, ccols, coarse, faces,
):
    step = pl.program_id(0)

    @pl.when(step == 0)
    def _():
        low[L] = jnp.zeros((E, E, C), f32)
        high[L] = jnp.zeros((E, E, C), f32)
        chigh[...] = jnp.zeros((L + 1, 4, E, C), f32)

        @pl.loop(0, L)
        def _(leaf):
            low[leaf] = low_in[leaf].astype(f32).reshape(E, E, C)
            high[leaf] = high_in[leaf, 0:FACE].astype(f32).reshape(E, E, C)
            coarse[...] = high_in[leaf, FACE : FACE + 16].astype(f32)
            for i in range(4):
                chigh[leaf, i, pl.ds(0, 4, stride=2), :] = coarse[4 * i : 4 * i + 4]

    for n in range(PER):
        leaf = PER * step + n
        for pair in range(5):
            for half in range(2):
                def store(at, value, n=n, pair=pair, half=half):
                    cols[n, pair, :, half * SPAN + at : half * SPAN + at + C] = value
                fill_plane(store, table, lines, low, high, leaf, 2 * pair + half, E)

            def store_coarse(at, value, n=n, pair=pair):
                ccols[n, pair, :, at : at + C] = value
            fill_plane(store_coarse, table, clines, None, chigh, leaf, pair + 1, 4)

        pre = pairs_dot(dot, cols, n, wa, wb)
        back = dot_turned(ccols[n, 0:4].reshape(4 * FACE, SPAN), wc[: 2 * C])
        back_next = dot_turned(ccols[n, 1:5].reshape(4 * FACE, SPAN), wc[2 * C :])
        sig = 1.0 / (1.0 + jnp.exp(-pre))
        slope = sig * (1.0 + pre * (1.0 - sig))
        for half in range(2):
            at = slice(half * C, half * C + C)
            m = half_planes(mask, leaf, half).astype(f32)
            h = m * pre[:, at] * sig[:, at]
            g = back[:, at] if half == 0 else back[:, at] + back_next
            d = g * m * slope[:, at]
            for pair in range(4):
                rows = slice(FACE * pair, FACE * pair + FACE)
                hidden[n, 2 * pair + half] = h[rows].astype(bf16)
                delta[n, 2 * pair + half] = d[rows].astype(bf16)
                faces[n, 0, 2 * pair + half] = h[rows]
                faces[n, 1, 2 * pair + half] = d[rows]
        for i in range(0, E, 2):
            def face(which, k, i=i, n=n):
                pair = [faces[n, which, i + m, pl.ds(k, E, stride=E), :] for m in range(2)]
                return jnp.concatenate(pair, axis=0).astype(bf16)
            rows = slice(E * i, E * i + 2 * E)
            up[0, n, rows] = face(0, E - 1)
            up[1, n, rows] = face(1, E - 1)
            down[n, rows] = face(1, 0)


def first_conv(table, lines, clines, mask, low, high, filters):
    def leafwise(*shape):
        return pl.BlockSpec((PER, *shape), lambda s: (s,) + (0,) * len(shape))

    return pl.pallas_call(
        first_kernel,
        grid=(L // PER,),
        out_shape=(
            jax.ShapeDtypeStruct((L, 5, FACE, 2 * SPAN), bf16),
            jax.ShapeDtypeStruct((L, E, FACE, C), bf16),
            jax.ShapeDtypeStruct((L, E, FACE, C), bf16),
            jax.ShapeDtypeStruct((2, L, FACE, C), bf16),
            jax.ShapeDtypeStruct((L, FACE, C), bf16),
        ),
        in_specs=[smem()] + [vmem()] * 8,
        out_specs=(
            leafwise(5, FACE, 2 * SPAN),
            leafwise(E, FACE, C),
            leafwise(E, FACE, C),
            pl.BlockSpec((2, PER, FACE, C), lambda s: (0, s, 0, 0)),
            leafwise(FACE, C),
        ),
        scratch_shapes=[
            pltpu.VMEM((L + 1, E, E, C), f32),
            pltpu.VMEM((L + 1, E, E, C), f32),
            pltpu.VMEM((L + 1, 4, E, C), f32),
            pltpu.VMEM((PER, 5, FACE, SPAN), bf16),
            pltpu.VMEM((16, C), f32),
            pltpu.VMEM((PER, 2, E, FACE, C), f32),
        ],
        compiler_params=params(24),
        cost_estimate=cost(15e9, 18e6),
        name="first_conv",
    )(table, lines, clines, mask, low, high, *filters)


def split_halves(core, whole, kept, sent):
    mine = pl.multiple_of(core * HALF, HALF)
    theirs = pl.multiple_of(HALF - core * HALF, HALF)
    for t in range(TAPS):
        kept[t] = whole[t, pl.ds(mine, HALF), :]
        sent[t] = whole[t, pl.ds(theirs, HALF), :].astype(bf16)


def first_grad_kernel(cols, delta, kept, sent, turned, total, whole):
    @pl.loop(0, L)
    def _(leaf):
        for half in range(2):
            turned[half * C : half * C + C, pl.ds(pl.multiple_of(leaf * 256, 256), 256)] = half_planes(delta, leaf, half).T

    total[...] = jnp.zeros_like(total)
    for tile in range(9):
        lanes = range(256 * tile, 256 * tile + 256, C)
        for next_pair in range(2):
            rhs = cols[:, next_pair : next_pair + 4, :, 256 * tile : 256 * tile + 256].reshape(L * 4 * FACE, 256)
            for half in range(2):
                use = [lane for lane in lanes if 0 <= 2 * next_pair + lane // SPAN - half <= 2]
                if not use:
                    continue
                res = dot(turned[half * C : half * C + C, :], rhs)
                for lane in use:
                    p, o = 2 * next_pair + lane // SPAN - half, lane % SPAN
                    total[p, :, o : o + C] += res[:, lane - 256 * tile : lane - 256 * tile + C]

    for p in range(3):
        for t in range(9):
            whole[9 * p + t] = total[p, :, t * C : t * C + C].T
    split_halves(core_at(), whole, kept, sent)


def halves_shape():
    return jax.ShapeDtypeStruct((TAPS, HALF, C), f32), jax.ShapeDtypeStruct((TAPS, HALF, C), bf16)


def first_grad(cols, delta):
    return pl.pallas_call(
        first_grad_kernel,
        out_shape=halves_shape(),
        in_specs=[vmem(), vmem()],
        out_specs=(vmem(), vmem()),
        scratch_shapes=[
            pltpu.VMEM((2 * C, L * 256), bf16),
            pltpu.VMEM((3, C, SPAN), f32),
            pltpu.VMEM((TAPS, C, C), f32),
        ],
        compiler_params=params(16),
        cost_estimate=cost(6e9, 14e6),
        name="first_grad",
    )(cols, delta)


def second_kernel(
    table, hidden, low_in, cot, mask, w2,
    coarse, kept, sent,
    lines, low, cols, turned, total, whole, thin,
):
    lines[L] = jnp.zeros((E, FACE, C), f32)
    low[L] = jnp.zeros((E, E, C), f32)
    thin[0] = jnp.zeros((2 * FACE, C), f32)

    @pl.loop(0, L)
    def _(leaf):
        lines[leaf] = hidden[leaf].astype(f32)
        low[leaf] = low_in[leaf].astype(f32).reshape(E, E, C)

    w = w2[...].reshape(TAPS * C, C)

    @pl.loop(0, L)
    def _(leaf):
        for x in range(E + 1):
            parts = shifted_lines(table, lines, low, None, leaf, x, E, range(E + 1))
            for q in range(3):
                for r in range(3):
                    value = jnp.concatenate([parts[r][q + 2 * m] for m in range(4)], axis=0).astype(bf16)
                    at = (x % 2) * SPAN + (3 * q + r) * C
                    cols[leaf, x // 2, :, at : at + C] = value
        lo = cols[leaf, 0:4].reshape(2 * FACE, 2 * SPAN)
        hi = cols[leaf, 1:5, :, 0:SPAN].reshape(2 * FACE, SPAN)
        res = jnp.dot(lo, w[: 2 * SPAN], preferred_element_type=f32) + jnp.dot(hi, w[2 * SPAN :], preferred_element_type=f32)
        active = []
        for i in range(4):
            plane = mask[leaf, 2 * i].astype(f32)
            active += [plane[16 * j : 16 * j + E] for j in range(4)]
        active = jnp.concatenate(active, axis=0)
        thin[1] = res * active
        coarse[leaf] = thin[1, pl.ds(0, FACE, stride=2), :].astype(bf16)
        thin[0, pl.ds(0, FACE, stride=2), :] = cot[leaf].astype(f32)
        upstream = (thin[0] * active).astype(bf16)
        turned[:, pl.ds(pl.multiple_of(leaf * 128, 128), 128)] = upstream.T

    for tile in range(9):
        at = slice(256 * tile, 256 * tile + 256)
        total[:, at] = jnp.dot(turned[...], cols[:, 0:4, :, at].reshape(L * 2 * FACE, 256), preferred_element_type=f32)
    for tile in range(5):
        end = min(256 * tile + 256, SPAN)
        rhs = cols[:, 1:5, :, 256 * tile : end].reshape(L * 2 * FACE, end - 256 * tile)
        total[:, 2 * SPAN + 256 * tile : 2 * SPAN + end] = jnp.dot(turned[...], rhs, preferred_element_type=f32)
    for t in range(TAPS):
        whole[t] = total[:, t * C : t * C + C].T
    split_halves(core_at(), whole, kept, sent)


def second_conv(table, hidden, low, cot, mask, w2):
    return pl.pallas_call(
        second_kernel,
        out_shape=(jax.ShapeDtypeStruct((L, 64, C), bf16), *halves_shape()),
        in_specs=[smem()] + [vmem()] * 5,
        out_specs=(vmem(),) * 3,
        scratch_shapes=[
            pltpu.VMEM((L + 1, E, FACE, C), f32),
            pltpu.VMEM((L + 1, E, E, C), f32),
            pltpu.VMEM((L, 5, 32, 2 * SPAN), bf16),
            pltpu.VMEM((C, L * 128), bf16),
            pltpu.VMEM((C, 3 * SPAN), f32),
            pltpu.VMEM((TAPS, C, C), f32),
            pltpu.VMEM((2, 2 * FACE, C), f32),
        ],
        compiler_params=params(20),
        cost_estimate=cost(8e9, 6e6),
        name="second_conv",
    )(table, hidden, low, cot, mask, w2)


def adjoint_kernel(start, count, table, delta, mask, low_in, high_in, w, out, lines, low, high, cols, wa, wb):
    lines[L] = jnp.zeros((E, FACE, C), f32)
    low[L] = jnp.zeros((E, E, C), f32)
    high[L] = jnp.zeros((E, E, C), f32)

    @pl.loop(0, L)
    def _(leaf):
        lines[leaf] = delta[leaf].astype(f32)
        low[leaf] = low_in[leaf].astype(f32).reshape(E, E, C)
        high[leaf] = high_in[leaf].astype(f32).reshape(E, E, C)

    banded_turned(w, wa, wb)

    @pl.loop(0, count // PER)
    def _(step):
        for n in range(PER):
            leaf = start + PER * step + n
            for pair in range(5):
                for half in range(2):
                    def store(at, value, n=n, pair=pair, half=half):
                        cols[n, pair, :, half * SPAN + at : half * SPAN + at + C] = value
                    fill_plane(store, table, lines, low, high, leaf, 2 * pair + half, E)
            res = pairs_dot(dot_turned, cols, n, wa, wb)
            for half in range(2):
                m = half_planes(mask, leaf, half).astype(f32)
                value = (res[:, half * C : half * C + C] * m).astype(bf16)
                for pair in range(4):
                    out[PER * step + n, 2 * pair + half] = value[FACE * pair : FACE * pair + FACE]


def adjoint_conv(start, count, table, delta, mask, low, high, w):
    def kernel(*refs):
        adjoint_kernel(start, count, *refs)

    return pl.pallas_call(
        kernel,
        out_shape=jax.ShapeDtypeStruct((count, E, FACE, C), bf16),
        in_specs=[smem()] + [vmem()] * 5,
        out_specs=vmem(),
        scratch_shapes=[
            pltpu.VMEM((L + 1, E, FACE, C), f32),
            pltpu.VMEM((L + 1, E, E, C), f32),
            pltpu.VMEM((L + 1, E, E, C), f32),
            pltpu.VMEM((PER, 5, FACE, 2 * SPAN), bf16),
            pltpu.VMEM((2 * C, 2 * SPAN), bf16),
            pltpu.VMEM((2 * C, 2 * SPAN), bf16),
        ],
        compiler_params=params(16),
        cost_estimate=cost(10e9 * count / L, 6e6),
        name="first_adjoint",
    )(table, delta, mask, low, high, w)


def start_sum_kernel(kept1, got1, kept2, got2, own, *sends):
    mine = ring_at()
    for d in range(4):
        rows = pl.ds(pl.multiple_of(((mine + d) % 4) * PIECE, PIECE), PIECE)
        for t in range(2 * TAPS):
            kept, got, n = (kept1, got1, t) if t < TAPS else (kept2, got2, t - TAPS)
            value = kept[n, rows, :] + got[n, rows, :].astype(f32)
            if d == 0:
                own[t] = value
            else:
                sends[d - 1][t] = value.astype(bf16)


def start_sum(kept1, got1, kept2, got2):
    return pl.pallas_call(
        start_sum_kernel,
        out_shape=(jax.ShapeDtypeStruct((2 * TAPS, PIECE, C), f32),) + (jax.ShapeDtypeStruct((2 * TAPS, PIECE, C), bf16),) * 3,
        in_specs=[vmem()] * 4,
        out_specs=(vmem(),) * 4,
        compiler_params=params(12),
        cost_estimate=cost(1e6, 3e6),
        name="start_sum",
    )(kept1, got1, kept2, got2)


def next_sum_kernel(own, a, b, c, out):
    value = own[...] + a[...].astype(f32) + b[...].astype(f32) + c[...].astype(f32)
    out[0 : 2 * TAPS] = value.astype(bf16)
    out[2 * TAPS :] = jnp.zeros((out.shape[0] - 2 * TAPS, PIECE, C), bf16)


def next_sum(own, received, taps):
    return pl.pallas_call(
        next_sum_kernel,
        out_shape=jax.ShapeDtypeStruct((taps, PIECE, C), bf16),
        in_specs=[vmem()] * 4,
        out_specs=vmem(),
        compiler_params=params(8),
        cost_estimate=cost(1e6, 2e6),
        name="next_sum",
    )(own, *received)


def last_sum_kernel(factor, parts, out):
    total = parts[0].astype(f32)
    for n in range(1, parts.shape[0]):
        total = total + parts[n].astype(f32)
    total = (total * factor).astype(bf16)
    for n in range(parts.shape[0]):
        out[n] = total


def last_sum(parts, factor):
    def kernel(*refs):
        last_sum_kernel(factor, *refs)

    return pl.pallas_call(
        kernel,
        out_shape=jax.ShapeDtypeStruct(parts.shape, bf16),
        in_specs=[vmem()],
        out_specs=vmem(),
        compiler_params=params(8),
        cost_estimate=cost(1e6, 1e6),
        name="last_sum",
    )(parts)


def finish_kernel(*refs):
    mine, theirs, (first, second) = refs[0:4], refs[4:8], refs[8:10]
    at_y, at_x = lax.axis_index("scene") >> 1, lax.axis_index("leaf") & 3
    core = core_at()
    for parts, which in ((mine, core), (theirs, 1 - core)):
        at = jnp.where(which == 0, at_y, at_x)
        for d in range(4):
            row = pl.multiple_of(which * HALF + ((at - d) & 3) * PIECE, PIECE)
            for t in range(2 * TAPS):
                out, n = (first, t) if t < TAPS else (second, t - TAPS)
                out[n, pl.ds(row, PIECE), :] = parts[d][t].astype(f32)


def finish(pieces):
    return pl.pallas_call(
        finish_kernel,
        out_shape=(jax.ShapeDtypeStruct((TAPS, C, C), f32),) * 2,
        in_specs=[vmem()] * 8,
        out_specs=(vmem(),) * 2,
        compiler_params=params(12),
        cost_estimate=cost(1e6, 6e6),
        name="finish",
    )(*pieces)


def ring_orders(leaf_count):
    out = []
    for d in range(1, 4):
        pairs = []
        for leaf in range(leaf_count):
            for scene in range(8):
                z, x, y, core = leaf // 4, leaf % 4, scene // 2, scene % 2
                x, y = (x, (y + d) % 4) if core == 0 else ((x + d) % 4, y)
                pairs.append((leaf * 8 + scene, (z * 4 + x) * 8 + y * 2 + core))
        out.append(pairs)
    return out


def rest_groups(leaf_count):
    depth = leaf_count // 4
    first = [[(z * 4 + x) * 8 + 2 * y for z in range(depth) for x in range(4)] for y in range(4)]
    second = [[(z * 4 + x) * 8 + 2 * y + 1 for z in range(depth) for y in range(4)] for x in range(4)]
    return first + second


def passed(block, distance):
    count = lax.axis_size("leaf")
    return lax.ppermute(block, "leaf", [(i - distance, i) for i in range(count) if 0 <= i - distance < count])


def to_other_core(block):
    return lax.ppermute(block, "scene", [(i, i ^ 1) for i in range(lax.axis_size("scene"))])


def shards(features, weight_first, weight_second, cotangent, neighbours, voxel_mask):
    both = ("leaf", "scene")
    leaf_count, scene_count = lax.axis_size("leaf"), lax.axis_size("scene")
    feat = features[0].reshape(L, E, FACE, C)
    cot = cotangent[0].reshape(L, 64, C)
    table = neighbours[0]
    voxels = voxel_mask[0]

    up, down = first_faces(voxels, feat, cot)
    with jax.named_scope("faces_in"):
        low = passed(up, 1)
        high = passed(down, -1)
    voxels, _ = lax.optimization_barrier((voxels, down))
    mask, lines, clines, *filters = setup(voxels, feat, cot, weight_first, weight_second)
    cols, hidden, delta, up, down = first_conv(table, lines, clines, mask, low, high, filters)
    with jax.named_scope("faces_mid"):
        tops = passed(up, 1)
        bottom = passed(down, -1)
        tops, bottom = lax.optimization_barrier((tops, bottom))
    kept1, sent1 = first_grad(cols, delta)
    with jax.named_scope("sum_core"):
        got1 = to_other_core(sent1)
    coarse, kept2, sent2 = second_conv(table, hidden, tops[0], cot, mask, weight_second)
    with jax.named_scope("sum_core"):
        got2 = to_other_core(sent2)
    own, *sends = start_sum(kept1, got1, kept2, got2)
    orders, groups = ring_orders(leaf_count), rest_groups(leaf_count)
    per = -(-2 * TAPS // leaf_count)
    with jax.named_scope("sum_ring"):
        received = [lax.ppermute(s, both, o) for s, o in zip(sends, orders)]
    parts = next_sum(own, received, per * leaf_count).reshape(leaf_count, per * PIECE, C)
    with jax.named_scope("sum_rest"):
        parts = lax.all_to_all(parts, both, 0, 0, axis_index_groups=groups, tiled=True)
    parts = last_sum(parts, 1.0 / math.sqrt(leaf_count * scene_count * L * E**3))
    with jax.named_scope("gather_rest"):
        parts = lax.all_to_all(parts, both, 0, 0, axis_index_groups=groups, tiled=True)
    own = parts.reshape(per * leaf_count, PIECE, C)[: 2 * TAPS]
    with jax.named_scope("gather_ring"):
        received = [lax.ppermute(own, both, o) for o in orders]
    with jax.named_scope("gather_core"):
        theirs = [to_other_core(own)]
    delta, own = lax.optimization_barrier((delta, own))
    input_grad = adjoint_conv(0, L, table, delta, mask, tops[1], bottom, weight_first)
    input_grad, received = lax.optimization_barrier((input_grad, received))
    with jax.named_scope("gather_core"):
        theirs += [to_other_core(piece) for piece in received]
    grad_first, grad_second = finish([own, *received, *theirs])
    return (
        coarse.reshape(1, L, 4, 4, 4, C),
        input_grad.reshape(1, L, E, E, E, C),
        grad_first,
        grad_second,
    )


def solution(mesh):
    placed = (
        P("scene", "leaf", None, None, None, None),
        P(),
        P(),
        P("scene", "leaf", None, None, None, None),
        P("scene", "leaf", None),
        P("scene", "leaf", None),
    )
    return jax.shard_map(
        shards,
        mesh=mesh,
        in_specs=placed,
        out_specs=(
            P("scene", "leaf", None, None, None, None),
            P("scene", "leaf", None, None, None, None),
            P(),
            P(),
        ),
        check_vma=False,
    )
```

```python
import math

import jax
import jax.numpy as jnp
from jax import lax
from jax.experimental import pallas as pl
from jax.experimental.pallas import tpu as pltpu
from jax.sharding import PartitionSpec as P

bf16 = jnp.bfloat16
f32 = jnp.float32
C = 128
L = 8
E = 8
FACE = E * E
SPAN = 9 * C
TAPS = 27
HALF = C // 2
PIECE = 16


def core_at():
    return lax.axis_index("scene") & 1


def by_parity(body):
    odd = lax.axis_index("leaf") & 1
    for parity in range(2):
        @pl.when(odd == parity)
        def _(parity=parity):
            body(1 - parity, parity)


def ring_at():
    return jnp.where(core_at() == 0, lax.axis_index("scene") >> 1, lax.axis_index("leaf") & 3)


def smem():
    return pl.BlockSpec(memory_space=pltpu.SMEM)


def vmem():
    return pl.BlockSpec(memory_space=pltpu.VMEM)


def params(mebibytes):
    return pltpu.CompilerParams(vmem_limit_bytes=mebibytes * 1024 * 1024)


def cost(flops, size):
    return pl.CostEstimate(flops=int(flops), bytes_accessed=int(size), transcendentals=0)


def edge_row(face, block, i, j):
    return jnp.broadcast_to(face[block, i, pl.ds(j, 1), :], (E, C))


def source_plane(x, top):
    return -1 if x == 0 else 1 if x == top + 1 else 0, top - 1 if x == 0 else 0 if x == top + 1 else x - 1


def block_at(neighbours, leaf, a, b, c):
    d = 9 * a + 3 * b + c
    if d == 0:
        return leaf
    n = neighbours[leaf, 13 + d if d < 0 else 12 + d]
    return jnp.where(n < 0, L, n & (L - 1))


def shifted_lines(table, lines, low, high, leaf, x, top, rows):
    a, i = source_plane(x, top)
    ends = (-1, 0, 1)
    at = [[block_at(table, leaf, a, b, c) if (c < 0 and low is not None) or c == 0 or (c > 0 and high is not None) else None for c in ends] for b in ends]
    ids = lax.broadcasted_iota(jnp.int32, (E, C), 0)
    out = ([], [], [])
    for y in rows:
        b = 0 if y == 0 else 2 if y == E + 1 else 1
        j = E - 1 if y == 0 else 0 if y == E + 1 else y - 1
        line = lines[at[b][1], i, E * j : E * j + E]
        below = jnp.where(ids == 0, 0.0 if low is None else edge_row(low, at[b][0], i, j), pltpu.roll(line, 1, 0))
        above = pltpu.roll(line, E - 1, 0)
        if high is not None:
            above = jnp.where(ids == E - 1, edge_row(high, at[b][2], i, j), above)
        for r, part in enumerate((below, line, above)):
            out[r].append(part)
    return out


def fill_plane(store, *where):
    parts = shifted_lines(*where, range(E + 2))
    whole = [jnp.concatenate(part, axis=0) for part in parts]
    for q in range(3):
        for r in range(3):
            store((3 * q + r) * C, whole[r][E * q : E * q + FACE].astype(bf16))


def banded(weight, first, second):
    zero = jnp.zeros((SPAN, C), bf16)
    w = [weight[9 * s : 9 * s + 9].reshape(SPAN, C) for s in range(3)]
    first[:SPAN, :C] = w[0]
    first[:SPAN, C:] = zero
    first[SPAN:, :C] = w[1]
    first[SPAN:, C:] = w[0]
    second[:SPAN, :C] = w[2]
    second[:SPAN, C:] = w[1]
    second[SPAN:, :C] = zero
    second[SPAN:, C:] = w[2]


def banded_turned(weight, first, second):
    zero = jnp.zeros((C, SPAN), bf16)
    w = [jnp.concatenate([weight[TAPS - 1 - t] for t in range(9 * s, 9 * s + 9)], axis=1) for s in range(3)]
    first[:C, :SPAN] = w[0]
    first[C:, :SPAN] = zero
    first[:C, SPAN:] = w[1]
    first[C:, SPAN:] = w[0]
    second[:C, :SPAN] = w[2]
    second[C:, :SPAN] = w[1]
    second[:C, SPAN:] = zero
    second[C:, SPAN:] = w[2]


def dot(x, w):
    return jnp.dot(x, w, preferred_element_type=f32)


def dot_turned(x, w):
    return lax.dot_general(x, w, (((1,), (1,)), ((), ())), preferred_element_type=f32)


def pairs_dot(multiply, cols, at, first, second):
    lo = cols[at, 0:4].reshape(4 * FACE, 2 * SPAN)
    hi = cols[at, 1:5].reshape(4 * FACE, 2 * SPAN)
    return multiply(lo, first[...]) + multiply(hi, second[...])


def half_planes(ref, leaf, half):
    return jnp.concatenate([ref[leaf, 2 * pair + half] for pair in range(4)], axis=0)


def spread_mask(voxels, leaf):
    return jnp.broadcast_to(voxels[leaf : leaf + 1, :].astype(f32), (C, E**3)).T


def faces_kernel(voxels, feat, cot, one, two, spread, held, coarse):
    for leaf in range(L):
        whole = spread_mask(voxels, leaf)
        spread[...] = whole
        coarse[...] = cot[leaf].astype(f32)
        edge = coarse[pl.ds(0, 16, stride=4), :]
        active = jnp.concatenate([spread[pl.ds(2 * FACE * i, 4, stride=16), :] for i in range(4)], axis=0)
        held[...] = feat[leaf].reshape(E**3, C).astype(f32) * whole
        up = held[pl.ds(E - 1, FACE, stride=E), :].astype(bf16)
        down = held[pl.ds(0, FACE, stride=E), :].astype(bf16)

        def write(below, above, leaf=leaf, up=up, down=down, edge=edge, active=active):
            out = (one, two)
            out[above][leaf, 0:FACE] = up
            out[above][leaf, FACE : FACE + 16] = jnp.zeros((16, C), bf16)
            out[below][leaf, 0:FACE] = down
            out[below][leaf, FACE : FACE + 16] = (edge * active).astype(bf16)

        by_parity(write)


def first_faces(voxels, feat, cot):
    return pl.pallas_call(
        faces_kernel,
        out_shape=(jax.ShapeDtypeStruct((L, FACE + 16, C), bf16),) * 2,
        in_specs=[vmem()] * 3,
        out_specs=(vmem(),) * 2,
        scratch_shapes=[pltpu.VMEM((E**3, C), f32), pltpu.VMEM((E**3, C), f32), pltpu.VMEM((64, C), f32)],
        compiler_params=params(12),
        cost_estimate=cost(6e9, 8e6),
        name="first_faces",
    )(voxels, feat, cot)


def setup_kernel(voxels, feat, cot, w1, w2, mask, lines, clines, wa, wb, wc, spread, coarse):
    lines[L] = jnp.zeros((E, FACE, C), f32)
    clines[...] = jnp.zeros((L + 1, 4, FACE, C), f32)
    for leaf in range(L):
        whole = spread_mask(voxels, leaf)
        spread[...] = whole
        mask[leaf] = whole.reshape(E, FACE, C).astype(bf16)
        lines[leaf] = feat[leaf].astype(f32) * whole.reshape(E, FACE, C)
        coarse[...] = cot[leaf].astype(f32)
        for i in range(4):
            for j in range(4):
                clines[leaf, i, pl.ds(16 * j, 4, stride=2), :] = coarse[16 * i + 4 * j : 16 * i + 4 * j + 4]
            clines[leaf, i] = clines[leaf, i] * spread[2 * FACE * i : 2 * FACE * i + FACE]
    banded(w1, wa, wb)
    for n, p in enumerate((1, 2, 0)):
        for t in range(9):
            wc[n * C : n * C + C, t * C : t * C + C] = w2[9 * p + 8 - t]


def setup(voxels, feat, cot, w1, w2):
    return pl.pallas_call(
        setup_kernel,
        out_shape=(
            jax.ShapeDtypeStruct((L, E, FACE, C), bf16),
            jax.ShapeDtypeStruct((L + 1, E, FACE, C), f32),
            jax.ShapeDtypeStruct((L + 1, 4, FACE, C), f32),
            jax.ShapeDtypeStruct((2 * SPAN, 2 * C), bf16),
            jax.ShapeDtypeStruct((2 * SPAN, 2 * C), bf16),
            jax.ShapeDtypeStruct((3 * C, SPAN), bf16),
        ),
        in_specs=[vmem()] * 5,
        out_specs=(vmem(),) * 6,
        scratch_shapes=[pltpu.VMEM((E**3, C), f32), pltpu.VMEM((64, C), f32)],
        compiler_params=params(14),
        cost_estimate=cost(1e9, 8e6),
        name="setup",
    )(voxels, feat, cot, w1, w2)


def first_kernel(
    table, lines, clines, mask, one_in, two_in, wa, wb, wc,
    cols, hidden, delta, one, two,
    low, high, chigh, ccols, coarse, faces,
):
    low[L] = jnp.zeros((E, E, C), f32)
    high[L] = jnp.zeros((E, E, C), f32)
    chigh[...] = jnp.zeros((L + 1, 4, E, C), f32)

    def receive(below, above):
        low_in, high_in = (one_in, two_in)[below], (one_in, two_in)[above]
        for leaf in range(L):
            low[leaf] = low_in[leaf, 0:FACE].astype(f32).reshape(E, E, C)
            high[leaf] = high_in[leaf, 0:FACE].astype(f32).reshape(E, E, C)
            coarse[...] = high_in[leaf, FACE : FACE + 16].astype(f32)
            for i in range(4):
                chigh[leaf, i, pl.ds(0, 4, stride=2), :] = coarse[4 * i : 4 * i + 4]

    by_parity(receive)

    for n in range(L):
        leaf = n
        for pair in range(5):
            for half in range(2):
                def store(at, value, n=n, pair=pair, half=half):
                    cols[n, pair, :, half * SPAN + at : half * SPAN + at + C] = value
                fill_plane(store, table, lines, low, high, leaf, 2 * pair + half, E)

            def store_coarse(at, value, n=n, pair=pair):
                ccols[n, pair, :, at : at + C] = value
            fill_plane(store_coarse, table, clines, None, chigh, leaf, pair + 1, 4)

        pre = pairs_dot(dot, cols, n, wa, wb)
        back = dot_turned(ccols[n, 0:4].reshape(4 * FACE, SPAN), wc[: 2 * C])
        back_next = dot_turned(ccols[n, 1:5].reshape(4 * FACE, SPAN), wc[2 * C :])
        sig = 1.0 / (1.0 + jnp.exp(-pre))
        slope = sig * (1.0 + pre * (1.0 - sig))
        for half in range(2):
            at = slice(half * C, half * C + C)
            m = half_planes(mask, leaf, half).astype(f32)
            h = m * pre[:, at] * sig[:, at]
            g = back[:, at] if half == 0 else back[:, at] + back_next
            d = g * m * slope[:, at]
            for pair in range(4):
                rows = slice(FACE * pair, FACE * pair + FACE)
                hidden[n, 2 * pair + half] = h[rows].astype(bf16)
                delta[n, 2 * pair + half] = d[rows].astype(bf16)
                faces[n, 0, 2 * pair + half] = h[rows]
                faces[n, 1, 2 * pair + half] = d[rows]

    def send(below, above):
        up, down = (one, two)[above], (one, two)[below]
        for n in range(L):
            for i in range(0, E, 2):
                def face(which, k):
                    pair = [faces[n, which, i + m, pl.ds(k, E, stride=E), :] for m in range(2)]
                    return jnp.concatenate(pair, axis=0).astype(bf16)
                rows = slice(E * i, E * i + 2 * E)
                up[0, n, rows] = face(0, E - 1)
                up[1, n, rows] = face(1, E - 1)
                down[0, n, rows] = face(1, 0)
                down[1, n, rows] = jnp.zeros((2 * E, C), bf16)

    by_parity(send)


def first_conv(table, lines, clines, mask, faces, filters):
    return pl.pallas_call(
        first_kernel,
        out_shape=(
            jax.ShapeDtypeStruct((L, 5, FACE, 2 * SPAN), bf16),
            jax.ShapeDtypeStruct((L, E, FACE, C), bf16),
            jax.ShapeDtypeStruct((L, E, FACE, C), bf16),
            jax.ShapeDtypeStruct((2, L, FACE, C), bf16),
            jax.ShapeDtypeStruct((2, L, FACE, C), bf16),
        ),
        in_specs=[smem()] + [vmem()] * 8,
        out_specs=(vmem(),) * 5,
        scratch_shapes=[
            pltpu.VMEM((L + 1, E, E, C), f32),
            pltpu.VMEM((L + 1, E, E, C), f32),
            pltpu.VMEM((L + 1, 4, E, C), f32),
            pltpu.VMEM((L, 5, FACE, SPAN), bf16),
            pltpu.VMEM((16, C), f32),
            pltpu.VMEM((L, 2, E, FACE, C), f32),
        ],
        compiler_params=params(24),
        cost_estimate=cost(15e9, 18e6),
        name="first_conv",
    )(table, lines, clines, mask, *faces, *filters)


def split_halves(core, whole, kept, sent):
    mine = pl.multiple_of(core * HALF, HALF)
    theirs = pl.multiple_of(HALF - core * HALF, HALF)
    for t in range(TAPS):
        kept[t] = whole[t, pl.ds(mine, HALF), :]
        sent[t] = whole[t, pl.ds(theirs, HALF), :].astype(bf16)


def first_grad_kernel(cols, delta, kept, sent, turned, total, whole):
    @pl.loop(0, L)
    def _(leaf):
        for half in range(2):
            turned[half * C : half * C + C, pl.ds(pl.multiple_of(leaf * 256, 256), 256)] = half_planes(delta, leaf, half).T

    total[...] = jnp.zeros_like(total)
    for tile in range(9):
        lanes = range(256 * tile, 256 * tile + 256, C)
        for next_pair in range(2):
            rhs = cols[:, next_pair : next_pair + 4, :, 256 * tile : 256 * tile + 256].reshape(L * 4 * FACE, 256)
            for half in range(2):
                use = [lane for lane in lanes if 0 <= 2 * next_pair + lane // SPAN - half <= 2]
                if not use:
                    continue
                res = dot(turned[half * C : half * C + C, :], rhs)
                for lane in use:
                    p, o = 2 * next_pair + lane // SPAN - half, lane % SPAN
                    total[p, :, o : o + C] += res[:, lane - 256 * tile : lane - 256 * tile + C]

    for p in range(3):
        for t in range(9):
            whole[9 * p + t] = total[p, :, t * C : t * C + C].T
    split_halves(core_at(), whole, kept, sent)


def halves_shape():
    return jax.ShapeDtypeStruct((TAPS, HALF, C), f32), jax.ShapeDtypeStruct((TAPS, HALF, C), bf16)


def first_grad(cols, delta):
    return pl.pallas_call(
        first_grad_kernel,
        out_shape=halves_shape(),
        in_specs=[vmem(), vmem()],
        out_specs=(vmem(), vmem()),
        scratch_shapes=[
            pltpu.VMEM((2 * C, L * 256), bf16),
            pltpu.VMEM((3, C, SPAN), f32),
            pltpu.VMEM((TAPS, C, C), f32),
        ],
        compiler_params=params(16),
        cost_estimate=cost(6e9, 14e6),
        name="first_grad",
    )(cols, delta)


def second_kernel(
    table, hidden, one_in, two_in, cot, mask, sent_first,
    cols, active_out, kept, sent,
    lines, low, turned, total, whole, thin,
):
    lines[L] = jnp.zeros((E, FACE, C), f32)
    low[L] = jnp.zeros((E, E, C), f32)
    thin[...] = jnp.zeros_like(thin)

    @pl.loop(0, L)
    def _(leaf):
        lines[leaf] = hidden[leaf].astype(f32)

    def receive(below, above):
        for leaf in range(L):
            low[leaf] = (one_in, two_in)[below][0, leaf].astype(f32).reshape(E, E, C)

    by_parity(receive)

    for leaf in range(L):
        for x in range(E + 1):
            parts = shifted_lines(table, lines, low, None, leaf, x, E, range(E + 1))
            for q in range(3):
                for r in range(3):
                    value = jnp.concatenate([parts[r][q + 2 * m] for m in range(4)], axis=0).astype(bf16)
                    at = (x % 2) * SPAN + (3 * q + r) * C
                    cols[leaf, x // 2, :, at : at + C] = value
        active = []
        for i in range(4):
            plane = mask[leaf, 2 * i].astype(f32)
            active += [plane[16 * j : 16 * j + E] for j in range(4)]
        active = jnp.concatenate(active, axis=0)
        active_out[leaf] = active.astype(bf16)
        thin[leaf, pl.ds(0, FACE, stride=2), :] = cot[leaf].astype(f32)
        upstream = (thin[leaf] * active).astype(bf16)
        turned[:, 128 * leaf : 128 * leaf + 128] = upstream.T

    for tile in range(9):
        at = slice(256 * tile, 256 * tile + 256)
        total[:, at] = jnp.dot(turned[...], cols[:, 0:4, :, at].reshape(L * 2 * FACE, 256), preferred_element_type=f32)
    for tile in range(5):
        end = min(256 * tile + 256, SPAN)
        rhs = cols[:, 1:5, :, 256 * tile : end].reshape(L * 2 * FACE, end - 256 * tile)
        total[:, 2 * SPAN + 256 * tile : 2 * SPAN + end] = jnp.dot(turned[...], rhs, preferred_element_type=f32)
    for t in range(TAPS):
        whole[t] = total[:, t * C : t * C + C].T
    sent[0:TAPS] = sent_first[...]
    split_halves(core_at(), whole, kept, sent.at[TAPS:])


def second_grad(table, hidden, faces, cot, mask, sent_first):
    return pl.pallas_call(
        second_kernel,
        out_shape=(
            jax.ShapeDtypeStruct((L, 5, 32, 2 * SPAN), bf16),
            jax.ShapeDtypeStruct((L, 2 * FACE, C), bf16),
            jax.ShapeDtypeStruct((TAPS, HALF, C), f32),
            jax.ShapeDtypeStruct((2 * TAPS, HALF, C), bf16),
        ),
        in_specs=[smem()] + [vmem()] * 6,
        out_specs=(vmem(),) * 4,
        scratch_shapes=[
            pltpu.VMEM((L + 1, E, FACE, C), f32),
            pltpu.VMEM((L + 1, E, E, C), f32),
            pltpu.VMEM((C, L * 128), bf16),
            pltpu.VMEM((C, 3 * SPAN), f32),
            pltpu.VMEM((TAPS, C, C), f32),
            pltpu.VMEM((L, 2 * FACE, C), f32),
        ],
        compiler_params=params(20),
        cost_estimate=cost(8e9, 6e6),
        name="second_grad",
    )(table, hidden, *faces, cot, mask, sent_first)


def coarse_kernel(cols, active, w2, coarse, thin):
    w = w2[...].reshape(TAPS * C, C)
    for leaf in range(L):
        lo = cols[leaf, 0:4].reshape(2 * FACE, 2 * SPAN)
        hi = cols[leaf, 1:5, :, 0:SPAN].reshape(2 * FACE, SPAN)
        thin[leaf] = (dot(lo, w[: 2 * SPAN]) + dot(hi, w[2 * SPAN :])) * active[leaf].astype(f32)
        coarse[leaf] = thin[leaf, pl.ds(0, FACE, stride=2), :].astype(bf16)


def coarse_conv(cols, active, w2):
    return pl.pallas_call(
        coarse_kernel,
        out_shape=jax.ShapeDtypeStruct((L, 64, C), bf16),
        in_specs=[vmem()] * 3,
        out_specs=vmem(),
        scratch_shapes=[pltpu.VMEM((L, 2 * FACE, C), f32)],
        compiler_params=params(12),
        cost_estimate=cost(1e9, 2e6),
        name="coarse_conv",
    )(cols, active, w2)


def adjoint_kernel(start, count, table, delta, mask, one_in, two_in, w, out, lines, low, high, cols, wa, wb):
    lines[L] = jnp.zeros((E, FACE, C), f32)
    low[L] = jnp.zeros((E, E, C), f32)
    high[L] = jnp.zeros((E, E, C), f32)

    @pl.loop(0, L)
    def _(leaf):
        lines[leaf] = delta[leaf].astype(f32)

    def receive(below, above):
        for leaf in range(L):
            low[leaf] = (one_in, two_in)[below][1, leaf].astype(f32).reshape(E, E, C)
            high[leaf] = (one_in, two_in)[above][0, leaf].astype(f32).reshape(E, E, C)

    by_parity(receive)

    banded_turned(w, wa, wb)

    for n in range(count):
        leaf = start + n
        for pair in range(5):
            for half in range(2):
                def store(at, value, n=n, pair=pair, half=half):
                    cols[n, pair, :, half * SPAN + at : half * SPAN + at + C] = value
                fill_plane(store, table, lines, low, high, leaf, 2 * pair + half, E)
        res = pairs_dot(dot_turned, cols, n, wa, wb)
        for half in range(2):
            m = half_planes(mask, leaf, half).astype(f32)
            value = (res[:, half * C : half * C + C] * m).astype(bf16)
            for pair in range(4):
                out[n, 2 * pair + half] = value[FACE * pair : FACE * pair + FACE]


def adjoint_conv(start, count, table, delta, mask, faces, w):
    def kernel(*refs):
        adjoint_kernel(start, count, *refs)

    return pl.pallas_call(
        kernel,
        out_shape=jax.ShapeDtypeStruct((count, E, FACE, C), bf16),
        in_specs=[smem()] + [vmem()] * 5,
        out_specs=vmem(),
        scratch_shapes=[
            pltpu.VMEM((L + 1, E, FACE, C), f32),
            pltpu.VMEM((L + 1, E, E, C), f32),
            pltpu.VMEM((L + 1, E, E, C), f32),
            pltpu.VMEM((count, 5, FACE, 2 * SPAN), bf16),
            pltpu.VMEM((2 * C, 2 * SPAN), bf16),
            pltpu.VMEM((2 * C, 2 * SPAN), bf16),
        ],
        compiler_params=params(26),
        cost_estimate=cost(10e9 * count / L, 6e6),
        name="first_adjoint",
    )(table, delta, mask, *faces, w)


def start_sum_kernel(kept1, kept2, got, own, *sends):
    mine = ring_at()
    for d in range(4):
        rows = pl.ds(pl.multiple_of((mine ^ d) * PIECE, PIECE), PIECE)
        for t in range(2 * TAPS):
            kept, n = (kept1, t) if t < TAPS else (kept2, t - TAPS)
            value = kept[n, rows, :] + got[t, rows, :].astype(f32)
            if d == 0:
                own[t] = value
            else:
                sends[d - 1][t] = value.astype(bf16)


def start_sum(kept1, kept2, got):
    return pl.pallas_call(
        start_sum_kernel,
        out_shape=(jax.ShapeDtypeStruct((2 * TAPS, PIECE, C), f32),) + (jax.ShapeDtypeStruct((2 * TAPS, PIECE, C), bf16),) * 3,
        in_specs=[vmem()] * 3,
        out_specs=(vmem(),) * 4,
        compiler_params=params(12),
        cost_estimate=cost(1e6, 3e6),
        name="start_sum",
    )(kept1, kept2, got)


def next_sum_kernel(own, a, b, c, out):
    value = own[...] + a[...].astype(f32) + b[...].astype(f32) + c[...].astype(f32)
    out[0 : 2 * TAPS] = value.astype(bf16)
    out[2 * TAPS :] = jnp.zeros((out.shape[0] - 2 * TAPS, PIECE, C), bf16)


def next_sum(own, received, taps):
    return pl.pallas_call(
        next_sum_kernel,
        out_shape=jax.ShapeDtypeStruct((taps, PIECE, C), bf16),
        in_specs=[vmem()] * 4,
        out_specs=vmem(),
        compiler_params=params(8),
        cost_estimate=cost(1e6, 2e6),
        name="next_sum",
    )(own, *received)


def last_sum_kernel(factor, parts, out):
    total = parts[0].astype(f32)
    for n in range(1, parts.shape[0]):
        total = total + parts[n].astype(f32)
    total = (total * factor).astype(bf16)
    for n in range(parts.shape[0]):
        out[n] = total


def last_sum(parts, factor):
    def kernel(*refs):
        last_sum_kernel(factor, *refs)

    return pl.pallas_call(
        kernel,
        out_shape=jax.ShapeDtypeStruct(parts.shape, bf16),
        in_specs=[vmem()],
        out_specs=vmem(),
        compiler_params=params(8),
        cost_estimate=cost(1e6, 1e6),
        name="last_sum",
    )(parts)


def finish_kernel(*refs):
    mine, theirs, (first, second) = refs[0:4], refs[4:8], refs[8:10]
    at_y, at_x = lax.axis_index("scene") >> 1, lax.axis_index("leaf") & 3
    core = core_at()
    for parts, which in ((mine, core), (theirs, 1 - core)):
        at = jnp.where(which == 0, at_y, at_x)
        for d in range(4):
            row = pl.multiple_of(which * HALF + (at ^ d) * PIECE, PIECE)
            for t in range(2 * TAPS):
                out, n = (first, t) if t < TAPS else (second, t - TAPS)
                out[n, pl.ds(row, PIECE), :] = parts[d][t].astype(f32)


def finish(pieces):
    return pl.pallas_call(
        finish_kernel,
        out_shape=(jax.ShapeDtypeStruct((TAPS, C, C), f32),) * 2,
        in_specs=[vmem()] * 8,
        out_specs=(vmem(),) * 2,
        compiler_params=params(12),
        cost_estimate=cost(1e6, 6e6),
        name="finish",
    )(*pieces)


def ring_orders(leaf_count):
    out = []
    for d in range(1, 4):
        pairs = []
        for leaf in range(leaf_count):
            for scene in range(8):
                z, x, y, core = leaf // 4, leaf % 4, scene // 2, scene % 2
                x, y = (x, y ^ d) if core == 0 else (x ^ d, y)
                pairs.append((leaf * 8 + scene, (z * 4 + x) * 8 + y * 2 + core))
        out.append(pairs)
    return out


def rest_groups(leaf_count):
    depth = leaf_count // 4
    first = [[(z * 4 + x) * 8 + 2 * y for z in range(depth) for x in range(4)] for y in range(4)]
    second = [[(z * 4 + x) * 8 + 2 * y + 1 for z in range(depth) for y in range(4)] for x in range(4)]
    return first + second


def exchanged(first, second):
    count = lax.axis_size("leaf")
    pairs = [(i, i ^ 1) for i in range(count)]
    shifted = [(i, i + 1 if i % 2 else i - 1) for i in range(1, count - 1)]
    return lax.ppermute(first, "leaf", pairs), lax.ppermute(second, "leaf", shifted)


def to_other_core(block):
    return lax.ppermute(block, "scene", [(i, i ^ 1) for i in range(lax.axis_size("scene"))])


def shards(features, weight_first, weight_second, cotangent, neighbours, voxel_mask):
    both = ("leaf", "scene")
    leaf_count, scene_count = lax.axis_size("leaf"), lax.axis_size("scene")
    feat = features[0].reshape(L, E, FACE, C)
    cot = cotangent[0].reshape(L, 64, C)
    table = neighbours[0]
    voxels = voxel_mask[0]

    one, two = first_faces(voxels, feat, cot)
    with jax.named_scope("faces_in"):
        faces = exchanged(one, two)
    voxels, _ = lax.optimization_barrier((voxels, one))
    mask, lines, clines, *filters = setup(voxels, feat, cot, weight_first, weight_second)
    cols, hidden, delta, one, two = first_conv(table, lines, clines, mask, faces, filters)
    with jax.named_scope("faces_mid"):
        faces = exchanged(one, two)
    kept1, sent1 = first_grad(cols, delta)
    cols2, active, kept2, sent = second_grad(table, hidden, faces, cot, mask, sent1)
    with jax.named_scope("sum_core"):
        got = to_other_core(sent)
    own, *sends = start_sum(kept1, kept2, got)
    orders, groups = ring_orders(leaf_count), rest_groups(leaf_count)
    per = -(-2 * TAPS // leaf_count)
    with jax.named_scope("sum_ring"):
        received = [lax.ppermute(s, both, o) for s, o in zip(sends, orders)]
    input_grad = adjoint_conv(0, L, table, delta, mask, faces, weight_first)
    own, input_grad = lax.optimization_barrier((own, input_grad))
    parts = next_sum(own, received, per * leaf_count).reshape(leaf_count, per * PIECE, C)
    with jax.named_scope("sum_rest"):
        parts = lax.all_to_all(parts, both, 0, 0, axis_index_groups=groups, tiled=True)
    parts = last_sum(parts, 1.0 / math.sqrt(leaf_count * scene_count * L * E**3))
    with jax.named_scope("gather_rest"):
        parts = lax.all_to_all(parts, both, 0, 0, axis_index_groups=groups, tiled=True)
    own = parts.reshape(per * leaf_count, PIECE, C)[: 2 * TAPS]
    with jax.named_scope("gather_ring"):
        received = [lax.ppermute(own, both, o) for o in orders]
    cols2, own = lax.optimization_barrier((cols2, own))
    coarse = coarse_conv(cols2, active, weight_second)
    coarse, mine = lax.optimization_barrier((coarse, [own, *received]))
    with jax.named_scope("gather_core"):
        theirs = [to_other_core(piece) for piece in mine]
    grad_first, grad_second = finish([*mine, *theirs])
    return (
        coarse.reshape(1, L, 4, 4, 4, C),
        input_grad.reshape(1, L, E, E, E, C),
        grad_first,
        grad_second,
    )


def solution(mesh):
    placed = (
        P("scene", "leaf", None, None, None, None),
        P(),
        P(),
        P("scene", "leaf", None, None, None, None),
        P("scene", "leaf", None),
        P("scene", "leaf", None),
    )
    return jax.shard_map(
        shards,
        mesh=mesh,
        in_specs=placed,
        out_specs=(
            P("scene", "leaf", None, None, None, None),
            P("scene", "leaf", None, None, None, None),
            P(),
            P(),
        ),
        check_vma=False,
    )
```

```python
import math

import jax
import jax.numpy as jnp
from jax import lax
from jax.experimental import pallas as pl
from jax.experimental.pallas import tpu as pltpu
from jax.sharding import PartitionSpec as P

bf16 = jnp.bfloat16
f32 = jnp.float32
C = 128
L = 8
E = 8
FACE = E * E
SPAN = 9 * C
TAPS = 27
HALF = C // 2
TOGETHER = 2
PIECE = 16


def core_at():
    return lax.axis_index("scene") & 1


def by_parity(body):
    odd = lax.axis_index("leaf") & 1
    for parity in range(2):
        @pl.when(odd == parity)
        def _(parity=parity):
            body(1 - parity, parity)


def ring_at():
    return jnp.where(core_at() == 0, lax.axis_index("scene") >> 1, lax.axis_index("leaf") & 3)


def smem():
    return pl.BlockSpec(memory_space=pltpu.SMEM)


def vmem():
    return pl.BlockSpec(memory_space=pltpu.VMEM)


def params(mebibytes):
    return pltpu.CompilerParams(vmem_limit_bytes=mebibytes * 1024 * 1024)


def cost(flops, size):
    return pl.CostEstimate(flops=int(flops), bytes_accessed=int(size), transcendentals=0)


def edge_row(face, block, i, j):
    return jnp.broadcast_to(face[block, i, pl.ds(j, 1), :], (E, C))


def source_plane(x, top):
    return -1 if x == 0 else 1 if x == top + 1 else 0, top - 1 if x == 0 else 0 if x == top + 1 else x - 1


def block_at(neighbours, leaf, a, b, c):
    d = 9 * a + 3 * b + c
    if d == 0:
        return leaf
    n = neighbours[leaf, 13 + d if d < 0 else 12 + d]
    return jnp.where(n < 0, L, n & (L - 1))


def shifted_lines(table, lines, low, high, leaf, x, top, rows):
    a, i = source_plane(x, top)
    ends = (-1, 0, 1)
    at = [[block_at(table, leaf, a, b, c) if (c < 0 and low is not None) or c == 0 or (c > 0 and high is not None) else None for c in ends] for b in ends]
    ids = lax.broadcasted_iota(jnp.int32, (E, C), 0)
    out = ([], [], [])
    for y in rows:
        b = 0 if y == 0 else 2 if y == E + 1 else 1
        j = E - 1 if y == 0 else 0 if y == E + 1 else y - 1
        line = lines[at[b][1], i, E * j : E * j + E]
        below = jnp.where(ids == 0, 0.0 if low is None else edge_row(low, at[b][0], i, j), pltpu.roll(line, 1, 0))
        above = pltpu.roll(line, E - 1, 0)
        if high is not None:
            above = jnp.where(ids == E - 1, edge_row(high, at[b][2], i, j), above)
        for r, part in enumerate((below, line, above)):
            out[r].append(part)
    return out


def fill_plane(store, *where):
    parts = shifted_lines(*where, range(E + 2))
    whole = [jnp.concatenate(part, axis=0) for part in parts]
    for q in range(3):
        for r in range(3):
            store((3 * q + r) * C, whole[r][E * q : E * q + FACE].astype(bf16))


def banded(weight, first, second):
    zero = jnp.zeros((SPAN, C), bf16)
    w = [weight[9 * s : 9 * s + 9].reshape(SPAN, C) for s in range(3)]
    first[:SPAN, :C] = w[0]
    first[:SPAN, C:] = zero
    first[SPAN:, :C] = w[1]
    first[SPAN:, C:] = w[0]
    second[:SPAN, :C] = w[2]
    second[:SPAN, C:] = w[1]
    second[SPAN:, :C] = zero
    second[SPAN:, C:] = w[2]


def banded_turned(weight, first, second):
    zero = jnp.zeros((C, SPAN), bf16)
    w = [jnp.concatenate([weight[TAPS - 1 - t] for t in range(9 * s, 9 * s + 9)], axis=1) for s in range(3)]
    first[:C, :SPAN] = w[0]
    first[C:, :SPAN] = zero
    first[:C, SPAN:] = w[1]
    first[C:, SPAN:] = w[0]
    second[:C, :SPAN] = w[2]
    second[C:, :SPAN] = w[1]
    second[:C, SPAN:] = zero
    second[C:, SPAN:] = w[2]


def dot(x, w):
    return jnp.dot(x, w, preferred_element_type=f32)


def dot_turned(x, w):
    return lax.dot_general(x, w, (((1,), (1,)), ((), ())), preferred_element_type=f32)


def pairs_dot(multiply, cols, at, first, second):
    lo = cols[at : at + TOGETHER, 0:4].reshape(TOGETHER * 4 * FACE, 2 * SPAN)
    hi = cols[at : at + TOGETHER, 1:5].reshape(TOGETHER * 4 * FACE, 2 * SPAN)
    return multiply(lo, first[...]) + multiply(hi, second[...])


def half_planes(ref, leaf, half):
    return jnp.concatenate([ref[leaf, 2 * pair + half] for pair in range(4)], axis=0)


def spread_mask(voxels, leaf):
    return jnp.broadcast_to(voxels[leaf : leaf + 1, :].astype(f32), (C, E**3)).T


def faces_kernel(voxels, feat, cot, one, two, spread, held, coarse):
    for leaf in range(L):
        whole = spread_mask(voxels, leaf)
        spread[...] = whole
        coarse[...] = cot[leaf].astype(f32)
        edge = coarse[pl.ds(0, 16, stride=4), :]
        active = jnp.concatenate([spread[pl.ds(2 * FACE * i, 4, stride=16), :] for i in range(4)], axis=0)
        held[...] = feat[leaf].reshape(E**3, C).astype(f32) * whole
        up = held[pl.ds(E - 1, FACE, stride=E), :].astype(bf16)
        down = held[pl.ds(0, FACE, stride=E), :].astype(bf16)

        def write(below, above, leaf=leaf, up=up, down=down, edge=edge, active=active):
            out = (one, two)
            out[above][leaf, 0:FACE] = up
            out[above][leaf, FACE : FACE + 16] = jnp.zeros((16, C), bf16)
            out[below][leaf, 0:FACE] = down
            out[below][leaf, FACE : FACE + 16] = (edge * active).astype(bf16)

        by_parity(write)


def first_faces(voxels, feat, cot):
    return pl.pallas_call(
        faces_kernel,
        out_shape=(jax.ShapeDtypeStruct((L, FACE + 16, C), bf16),) * 2,
        in_specs=[vmem()] * 3,
        out_specs=(vmem(),) * 2,
        scratch_shapes=[pltpu.VMEM((E**3, C), f32), pltpu.VMEM((E**3, C), f32), pltpu.VMEM((64, C), f32)],
        compiler_params=params(12),
        cost_estimate=cost(6e9, 8e6),
        name="first_faces",
    )(voxels, feat, cot)


def setup_kernel(voxels, feat, cot, w1, w2, mask, lines, clines, active, upturned, wa, wb, wc, thin):
    lines[L] = jnp.zeros((E, FACE, C), f32)
    clines[L] = jnp.zeros((4, 4 * E, C), f32)
    thin[...] = jnp.zeros_like(thin)
    for leaf in range(L):
        whole = spread_mask(voxels, leaf)
        mask[leaf] = whole.reshape(E, FACE, C).astype(bf16)
        lines[leaf] = feat[leaf].astype(f32) * whole.reshape(E, FACE, C)
        starts = [2 * FACE * i + 2 * E * j for i in range(4) for j in range(4)]
        kept = jnp.concatenate([whole[at : at + E] for at in starts], axis=0)
        active[leaf] = kept.astype(bf16)
        thin[leaf, pl.ds(0, FACE, stride=2), :] = cot[leaf].astype(f32)
        upstream = thin[leaf] * kept
        clines[leaf] = upstream.reshape(4, 4 * E, C)
        upturned[:, 2 * FACE * leaf : 2 * FACE * leaf + 2 * FACE] = upstream.astype(bf16).T
    banded(w1, wa, wb)
    for n, p in enumerate((1, 2, 0)):
        for m, q in enumerate((1, 2, 0)):
            for r in range(3):
                at = (3 * m + r) * C
                wc[n * C : n * C + C, at : at + C] = w2[9 * p + 3 * q + 2 - r]


def setup(voxels, feat, cot, w1, w2):
    return pl.pallas_call(
        setup_kernel,
        out_shape=(
            jax.ShapeDtypeStruct((L, E, FACE, C), bf16),
            jax.ShapeDtypeStruct((L + 1, E, FACE, C), f32),
            jax.ShapeDtypeStruct((L + 1, 4, 4 * E, C), f32),
            jax.ShapeDtypeStruct((L, 2 * FACE, C), bf16),
            jax.ShapeDtypeStruct((C, L * 2 * FACE), bf16),
            jax.ShapeDtypeStruct((2 * SPAN, 2 * C), bf16),
            jax.ShapeDtypeStruct((2 * SPAN, 2 * C), bf16),
            jax.ShapeDtypeStruct((3 * C, SPAN), bf16),
        ),
        in_specs=[vmem()] * 5,
        out_specs=(vmem(),) * 8,
        scratch_shapes=[pltpu.VMEM((L, 2 * FACE, C), f32)],
        compiler_params=params(14),
        cost_estimate=cost(1e9, 8e6),
        name="setup",
    )(voxels, feat, cot, w1, w2)


def fill_coarse(store, table, clines, chigh, leaf, x):
    a, i = (1, 0) if x == 4 else (0, x)
    ids = lax.broadcasted_iota(jnp.int32, (E, C), 0)
    out = ([], [], [])
    for y in range(5):
        b, j = (1, 0) if y == 4 else (0, y)
        line = clines[block_at(table, leaf, a, b, 0), i, E * j : E * j + E]
        beyond = chigh[block_at(table, leaf, a, b, 1), 4 * i + j : 4 * i + j + 1, :]
        above = jnp.where(ids == E - 1, jnp.broadcast_to(beyond, (E, C)), pltpu.roll(line, E - 1, 0))
        for r, part in enumerate((pltpu.roll(line, 1, 0), line, above)):
            out[r].append(part)
    for r in range(3):
        whole = jnp.concatenate(out[r], axis=0)
        store(r * C, whole[: 4 * E].astype(bf16))
        store((3 + r) * C, whole[E:].astype(bf16))


def first_kernel(
    table, lines, clines, mask, one_in, two_in, wa, wb, wc,
    cols, hidden, delta, turned, one, two,
    low, high, chigh, ccols,
):
    low[L] = jnp.zeros((E, E, C), f32)
    high[L] = jnp.zeros((E, E, C), f32)
    chigh[L] = jnp.zeros((16, C), f32)
    hidden[L] = jnp.zeros((E, FACE, C), f32)
    delta[L] = jnp.zeros((E, FACE, C), f32)

    def receive(below, above):
        low_in, high_in = (one_in, two_in)[below], (one_in, two_in)[above]
        for leaf in range(L):
            low[leaf] = low_in[leaf, 0:FACE].astype(f32).reshape(E, E, C)
            high[leaf] = high_in[leaf, 0:FACE].astype(f32).reshape(E, E, C)
            chigh[leaf] = high_in[leaf, FACE : FACE + 16].astype(f32)

    by_parity(receive)

    def fill(n):
        for pair in range(5):
            for half in range(2):
                def store(at, value, pair=pair, half=half):
                    cols[n, pair, :, half * SPAN + at : half * SPAN + at + C] = value
                fill_plane(store, table, lines, low, high, n, 2 * pair + half, E)

            def store_coarse(at, value, pair=pair):
                ccols[n, pair, :, at : at + C] = value
            fill_coarse(store_coarse, table, clines, chigh, n, pair)

    for base in range(0, L, TOGETHER):
        for n in range(base, base + TOGETHER):
            fill(n)
        pre_all = pairs_dot(dot, cols, base, wa, wb)
        here = ccols[base : base + TOGETHER, 0:4].reshape(TOGETHER * 128, 6 * C)
        there = ccols[base : base + TOGETHER, 1:5].reshape(TOGETHER * 128, 6 * C)
        even, odd = slice(0, 3 * C), slice(3 * C, 9 * C)
        back = [dot_turned(here[:, : 3 * C], wc[: 2 * C, even]), dot_turned(here, wc[: 2 * C, odd])]
        back_next = [dot_turned(there[:, : 3 * C], wc[2 * C :, even]), dot_turned(there, wc[2 * C :, odd])]
        for n in range(base, base + TOGETHER):
            pre = pre_all[4 * FACE * (n - base) : 4 * FACE * (n - base) + 4 * FACE]
            sig = 1.0 / (1.0 + jnp.exp(-pre))
            slope = sig * (1.0 + pre * (1.0 - sig))
            for half in range(2):
                at = slice(half * C, half * C + C)
                m = half_planes(mask, n, half).astype(f32)
                h = m * pre[:, at] * sig[:, at]
                parts = [back[o][:, at] if half == 0 else back[o][:, at] + back_next[o] for o in range(2)]
                first_row = 128 * (n - base)
                rows = range(first_row, first_row + 128, E)
                g = jnp.concatenate([parts[o][i : i + E] for i in rows for o in range(2)], axis=0)
                d = g * m * slope[:, at]
                for pair in range(4):
                    rows = slice(FACE * pair, FACE * pair + FACE)
                    hidden[n, 2 * pair + half] = h[rows]
                    delta[n, 2 * pair + half] = d[rows]
                turned[half * C : half * C + C, 256 * n : 256 * n + 256] = d.astype(bf16).T

    def send(below, above):
        up, down = (one, two)[above], (one, two)[below]
        for n in range(L):
            for i in range(0, E, 2):
                def face(ref, k):
                    pair = [ref[n, i + m, pl.ds(k, E, stride=E), :] for m in range(2)]
                    return jnp.concatenate(pair, axis=0).astype(bf16)
                rows = slice(E * i, E * i + 2 * E)
                up[0, n, rows] = face(hidden, E - 1)
                up[1, n, rows] = face(delta, E - 1)
                down[0, n, rows] = face(delta, 0)
                down[1, n, rows] = jnp.zeros((2 * E, C), bf16)

    by_parity(send)


def first_conv(table, lines, clines, mask, faces, filters):
    return pl.pallas_call(
        first_kernel,
        out_shape=(
            jax.ShapeDtypeStruct((L, 5, FACE, 2 * SPAN), bf16),
            jax.ShapeDtypeStruct((L + 1, E, FACE, C), f32),
            jax.ShapeDtypeStruct((L + 1, E, FACE, C), f32),
            jax.ShapeDtypeStruct((2 * C, L * 256), bf16),
            jax.ShapeDtypeStruct((2, L, FACE, C), bf16),
            jax.ShapeDtypeStruct((2, L, FACE, C), bf16),
        ),
        in_specs=[smem()] + [vmem()] * 8,
        out_specs=(vmem(),) * 6,
        scratch_shapes=[
            pltpu.VMEM((L + 1, E, E, C), f32),
            pltpu.VMEM((L + 1, E, E, C), f32),
            pltpu.VMEM((L + 1, 16, C), f32),
            pltpu.VMEM((L, 5, 32, 6 * C), bf16),
        ],
        compiler_params=params(20),
        cost_estimate=cost(15e9, 18e6),
        name="first_conv",
    )(table, lines, clines, mask, *faces, *filters)


def split_halves(core, whole, kept, sent):
    mine = pl.multiple_of(core * HALF, HALF)
    theirs = pl.multiple_of(HALF - core * HALF, HALF)
    for t in range(TAPS):
        kept[t] = whole[t, pl.ds(mine, HALF), :]
        sent[t] = whole[t, pl.ds(theirs, HALF), :].astype(bf16)


def first_grad_kernel(cols, turned, kept, sent, total, whole):
    total[...] = jnp.zeros_like(total)
    for tile in range(9):
        lanes = range(256 * tile, 256 * tile + 256, C)
        for next_pair in range(2):
            rhs = cols[:, next_pair : next_pair + 4, :, 256 * tile : 256 * tile + 256].reshape(L * 4 * FACE, 256)
            for half in range(2):
                use = [lane for lane in lanes if 0 <= 2 * next_pair + lane // SPAN - half <= 2]
                if not use:
                    continue
                res = dot(turned[half * C : half * C + C, :], rhs)
                for lane in use:
                    p, o = 2 * next_pair + lane // SPAN - half, lane % SPAN
                    total[p, :, o : o + C] += res[:, lane - 256 * tile : lane - 256 * tile + C]

    for p in range(3):
        for t in range(9):
            whole[9 * p + t] = total[p, :, t * C : t * C + C].T
    split_halves(core_at(), whole, kept, sent)


def halves_shape():
    return jax.ShapeDtypeStruct((TAPS, HALF, C), f32), jax.ShapeDtypeStruct((TAPS, HALF, C), bf16)


def first_grad(cols, turned):
    return pl.pallas_call(
        first_grad_kernel,
        out_shape=halves_shape(),
        in_specs=[vmem(), vmem()],
        out_specs=(vmem(), vmem()),
        scratch_shapes=[
            pltpu.VMEM((3, C, SPAN), f32),
            pltpu.VMEM((TAPS, C, C), f32),
        ],
        compiler_params=params(16),
        cost_estimate=cost(6e9, 14e6),
        name="first_grad",
    )(cols, turned)


def second_kernel(
    table, lines, one_in, two_in, turned, sent_first,
    cols, kept, sent,
    low, total, whole,
):
    low[L] = jnp.zeros((E, E, C), f32)

    def receive(below, above):
        for leaf in range(L):
            low[leaf] = (one_in, two_in)[below][0, leaf].astype(f32).reshape(E, E, C)

    by_parity(receive)

    for leaf in range(L):
        for x in range(E + 1):
            parts = shifted_lines(table, lines, low, None, leaf, x, E, range(E + 1))
            for q in range(3):
                for r in range(3):
                    value = jnp.concatenate([parts[r][q + 2 * m] for m in range(4)], axis=0).astype(bf16)
                    at = (x % 2) * SPAN + (3 * q + r) * C
                    cols[leaf, x // 2, :, at : at + C] = value

    for tile in range(9):
        at = slice(256 * tile, 256 * tile + 256)
        total[:, at] = jnp.dot(turned[...], cols[:, 0:4, :, at].reshape(L * 2 * FACE, 256), preferred_element_type=f32)
    for tile in range(5):
        end = min(256 * tile + 256, SPAN)
        rhs = cols[:, 1:5, :, 256 * tile : end].reshape(L * 2 * FACE, end - 256 * tile)
        total[:, 2 * SPAN + 256 * tile : 2 * SPAN + end] = jnp.dot(turned[...], rhs, preferred_element_type=f32)
    for t in range(TAPS):
        whole[t] = total[:, t * C : t * C + C].T
    sent[0:TAPS] = sent_first[...]
    split_halves(core_at(), whole, kept, sent.at[TAPS:])


def second_grad(table, hidden, faces, upturned, sent_first):
    return pl.pallas_call(
        second_kernel,
        out_shape=(
            jax.ShapeDtypeStruct((L, 5, 32, 2 * SPAN), bf16),
            jax.ShapeDtypeStruct((TAPS, HALF, C), f32),
            jax.ShapeDtypeStruct((2 * TAPS, HALF, C), bf16),
        ),
        in_specs=[smem()] + [vmem()] * 5,
        out_specs=(vmem(),) * 3,
        scratch_shapes=[
            pltpu.VMEM((L + 1, E, E, C), f32),
            pltpu.VMEM((C, 3 * SPAN), f32),
            pltpu.VMEM((TAPS, C, C), f32),
        ],
        compiler_params=params(14),
        cost_estimate=cost(8e9, 6e6),
        name="second_grad",
    )(table, hidden, *faces, upturned, sent_first)


def coarse_kernel(cols, active, w2, coarse, thin):
    w = w2[...].reshape(TAPS * C, C)
    for leaf in range(L):
        lo = cols[leaf, 0:4].reshape(2 * FACE, 2 * SPAN)
        hi = cols[leaf, 1:5, :, 0:SPAN].reshape(2 * FACE, SPAN)
        thin[leaf] = (dot(lo, w[: 2 * SPAN]) + dot(hi, w[2 * SPAN :])) * active[leaf].astype(f32)
        coarse[leaf] = thin[leaf, pl.ds(0, FACE, stride=2), :].astype(bf16)


def coarse_conv(cols, active, w2):
    return pl.pallas_call(
        coarse_kernel,
        out_shape=jax.ShapeDtypeStruct((L, 64, C), bf16),
        in_specs=[vmem()] * 3,
        out_specs=vmem(),
        scratch_shapes=[pltpu.VMEM((L, 2 * FACE, C), f32)],
        compiler_params=params(12),
        cost_estimate=cost(1e9, 2e6),
        name="coarse_conv",
    )(cols, active, w2)


def adjoint_kernel(start, count, table, lines, mask, one_in, two_in, w, out, low, high, cols, wa, wb):
    low[L] = jnp.zeros((E, E, C), f32)
    high[L] = jnp.zeros((E, E, C), f32)

    def receive(below, above):
        for leaf in range(L):
            low[leaf] = (one_in, two_in)[below][1, leaf].astype(f32).reshape(E, E, C)
            high[leaf] = (one_in, two_in)[above][0, leaf].astype(f32).reshape(E, E, C)

    by_parity(receive)

    banded_turned(w, wa, wb)

    for base in range(0, count, TOGETHER):
        for n in range(base, base + TOGETHER):
            for pair in range(5):
                for half in range(2):
                    def store(at, value, n=n, pair=pair, half=half):
                        cols[n, pair, :, half * SPAN + at : half * SPAN + at + C] = value
                    fill_plane(store, table, lines, low, high, start + n, 2 * pair + half, E)
        res_all = pairs_dot(dot_turned, cols, base, wa, wb)
        for n in range(base, base + TOGETHER):
            res = res_all[4 * FACE * (n - base) : 4 * FACE * (n - base) + 4 * FACE]
            for half in range(2):
                m = half_planes(mask, start + n, half).astype(f32)
                value = (res[:, half * C : half * C + C] * m).astype(bf16)
                for pair in range(4):
                    out[n, 2 * pair + half] = value[FACE * pair : FACE * pair + FACE]


def adjoint_conv(start, count, table, delta, mask, faces, w):
    def kernel(*refs):
        adjoint_kernel(start, count, *refs)

    return pl.pallas_call(
        kernel,
        out_shape=jax.ShapeDtypeStruct((count, E, FACE, C), bf16),
        in_specs=[smem()] + [vmem()] * 5,
        out_specs=vmem(),
        scratch_shapes=[
            pltpu.VMEM((L + 1, E, E, C), f32),
            pltpu.VMEM((L + 1, E, E, C), f32),
            pltpu.VMEM((count, 5, FACE, 2 * SPAN), bf16),
            pltpu.VMEM((2 * C, 2 * SPAN), bf16),
            pltpu.VMEM((2 * C, 2 * SPAN), bf16),
        ],
        compiler_params=params(26),
        cost_estimate=cost(10e9 * count / L, 6e6),
        name="first_adjoint",
    )(table, delta, mask, *faces, w)


def start_sum_kernel(kept1, kept2, got, own, *sends):
    mine = ring_at()
    for d in range(4):
        rows = pl.ds(pl.multiple_of((mine ^ d) * PIECE, PIECE), PIECE)
        for t in range(2 * TAPS):
            kept, n = (kept1, t) if t < TAPS else (kept2, t - TAPS)
            value = kept[n, rows, :] + got[t, rows, :].astype(f32)
            if d == 0:
                own[t] = value
            else:
                sends[3 - d][t] = value.astype(bf16)


def start_sum(kept1, kept2, got):
    return pl.pallas_call(
        start_sum_kernel,
        out_shape=(jax.ShapeDtypeStruct((2 * TAPS, PIECE, C), f32),) + (jax.ShapeDtypeStruct((2 * TAPS, PIECE, C), bf16),) * 3,
        in_specs=[vmem()] * 3,
        out_specs=(vmem(),) * 4,
        compiler_params=params(12),
        cost_estimate=cost(1e6, 3e6),
        name="start_sum",
    )(kept1, kept2, got)


def next_sum_kernel(own, a, b, c, out):
    value = own[...] + a[...].astype(f32) + b[...].astype(f32) + c[...].astype(f32)
    out[0 : 2 * TAPS] = value.astype(bf16)
    out[2 * TAPS :] = jnp.zeros((out.shape[0] - 2 * TAPS, PIECE, C), bf16)


def next_sum(own, received, taps):
    return pl.pallas_call(
        next_sum_kernel,
        out_shape=jax.ShapeDtypeStruct((taps, PIECE, C), bf16),
        in_specs=[vmem()] * 4,
        out_specs=vmem(),
        compiler_params=params(8),
        cost_estimate=cost(1e6, 2e6),
        name="next_sum",
    )(own, *received)


def last_sum_kernel(factor, parts, out):
    total = parts[0].astype(f32)
    for n in range(1, parts.shape[0]):
        total = total + parts[n].astype(f32)
    total = (total * factor).astype(bf16)
    for n in range(parts.shape[0]):
        out[n] = total


def last_sum(parts, factor):
    def kernel(*refs):
        last_sum_kernel(factor, *refs)

    return pl.pallas_call(
        kernel,
        out_shape=jax.ShapeDtypeStruct(parts.shape, bf16),
        in_specs=[vmem()],
        out_specs=vmem(),
        compiler_params=params(8),
        cost_estimate=cost(1e6, 1e6),
        name="last_sum",
    )(parts)


def finish_kernel(*refs):
    mine, theirs, (first, second) = refs[0:4], refs[4:8], refs[8:10]
    at_y, at_x = lax.axis_index("scene") >> 1, lax.axis_index("leaf") & 3
    core = core_at()
    for parts, which in ((mine, core), (theirs, 1 - core)):
        at = jnp.where(which == 0, at_y, at_x)
        for d in range(4):
            row = pl.multiple_of(which * HALF + (at ^ d) * PIECE, PIECE)
            for t in range(2 * TAPS):
                out, n = (first, t) if t < TAPS else (second, t - TAPS)
                out[n, pl.ds(row, PIECE), :] = parts[d][t].astype(f32)


def finish(pieces):
    return pl.pallas_call(
        finish_kernel,
        out_shape=(jax.ShapeDtypeStruct((TAPS, C, C), f32),) * 2,
        in_specs=[vmem()] * 8,
        out_specs=(vmem(),) * 2,
        compiler_params=params(12),
        cost_estimate=cost(1e6, 6e6),
        name="finish",
    )(*pieces)


def ring_orders(leaf_count):
    out = []
    for d in range(1, 4):
        pairs = []
        for leaf in range(leaf_count):
            for scene in range(8):
                z, x, y, core = leaf // 4, leaf % 4, scene // 2, scene % 2
                x, y = (x, y ^ d) if core == 0 else (x ^ d, y)
                pairs.append((leaf * 8 + scene, (z * 4 + x) * 8 + y * 2 + core))
        out.append(pairs)
    return out


def rest_groups(leaf_count):
    depth = leaf_count // 4
    first = [[(z * 4 + x) * 8 + 2 * y for z in range(depth) for x in range(4)] for y in range(4)]
    second = [[(z * 4 + x) * 8 + 2 * y + 1 for z in range(depth) for y in range(4)] for x in range(4)]
    return first + second


def exchanged(first, second):
    count = lax.axis_size("leaf")
    pairs = [(i, i ^ 1) for i in range(count)]
    shifted = [(i, i + 1 if i % 2 else i - 1) for i in range(1, count - 1)]
    return lax.ppermute(first, "leaf", pairs), lax.ppermute(second, "leaf", shifted)


def to_other_core(block):
    return lax.ppermute(block, "scene", [(i, i ^ 1) for i in range(lax.axis_size("scene"))])


def shards(features, weight_first, weight_second, cotangent, neighbours, voxel_mask):
    both = ("leaf", "scene")
    leaf_count, scene_count = lax.axis_size("leaf"), lax.axis_size("scene")
    feat = features[0].reshape(L, E, FACE, C)
    cot = cotangent[0].reshape(L, 64, C)
    table = neighbours[0]
    voxels = voxel_mask[0]

    one, two = first_faces(voxels, feat, cot)
    with jax.named_scope("faces_in"):
        faces = exchanged(one, two)
    voxels, _ = lax.optimization_barrier((voxels, one))
    mask, lines, clines, active, upturned, *filters = setup(voxels, feat, cot, weight_first, weight_second)
    cols, hidden, delta, turned, one, two = first_conv(table, lines, clines, mask, faces, filters)
    with jax.named_scope("faces_mid"):
        faces = exchanged(one, two)
    kept1, sent1 = first_grad(cols, turned)
    cols2, kept2, sent = second_grad(table, hidden, faces, upturned, sent1)
    with jax.named_scope("sum_core"):
        got = to_other_core(sent)
    own, *sends = start_sum(kept1, kept2, got)
    orders, groups = ring_orders(leaf_count), rest_groups(leaf_count)
    per = -(-2 * TAPS // leaf_count)
    with jax.named_scope("sum_ring"):
        received = [lax.ppermute(s, both, o) for s, o in zip(sends, orders[::-1])]
    input_grad = adjoint_conv(0, L, table, delta, mask, faces, weight_first)
    own, input_grad = lax.optimization_barrier((own, input_grad))
    parts = next_sum(own, received, per * leaf_count).reshape(leaf_count, per * PIECE, C)
    with jax.named_scope("sum_rest"):
        parts = lax.all_to_all(parts, both, 0, 0, axis_index_groups=groups, tiled=True)
    parts = last_sum(parts, 1.0 / math.sqrt(leaf_count * scene_count * L * E**3))
    with jax.named_scope("gather_rest"):
        parts = lax.all_to_all(parts, both, 0, 0, axis_index_groups=groups, tiled=True)
    own = parts.reshape(per * leaf_count, PIECE, C)[: 2 * TAPS]
    with jax.named_scope("gather_ring"):
        received = [lax.ppermute(own, both, o) for o in orders]
    cols2, own = lax.optimization_barrier((cols2, own))
    coarse = coarse_conv(cols2, active, weight_second)
    coarse, mine = lax.optimization_barrier((coarse, [own, *received]))
    with jax.named_scope("gather_core"):
        theirs = [to_other_core(piece) for piece in mine]
    grad_first, grad_second = finish([*mine, *theirs])
    return (
        coarse.reshape(1, L, 4, 4, 4, C),
        input_grad.reshape(1, L, E, E, E, C),
        grad_first,
        grad_second,
    )


def solution(mesh):
    placed = (
        P("scene", "leaf", None, None, None, None),
        P(),
        P(),
        P("scene", "leaf", None, None, None, None),
        P("scene", "leaf", None),
        P("scene", "leaf", None),
    )
    return jax.shard_map(
        shards,
        mesh=mesh,
        in_specs=placed,
        out_specs=(
            P("scene", "leaf", None, None, None, None),
            P("scene", "leaf", None, None, None, None),
            P(),
            P(),
        ),
        check_vma=False,
    )
```

```python
import math

import jax
import jax.numpy as jnp
from jax import lax
from jax.experimental import pallas as pl
from jax.experimental.pallas import tpu as pltpu
from jax.sharding import PartitionSpec as P

bf16 = jnp.bfloat16
f32 = jnp.float32
C = 128
L = 8
E = 8
FACE = E * E
SPAN = 9 * C
TAPS = 27
HALF = C // 2
TOGETHER = 2
PIECE = 16


def core_at():
    return lax.axis_index("scene") & 1


def by_parity(body):
    odd = lax.axis_index("leaf") & 1
    for parity in range(2):
        @pl.when(odd == parity)
        def _(parity=parity):
            body(1 - parity, parity)


def ring_at():
    return jnp.where(core_at() == 0, lax.axis_index("scene") >> 1, lax.axis_index("leaf") & 3)


def smem():
    return pl.BlockSpec(memory_space=pltpu.SMEM)


def vmem():
    return pl.BlockSpec(memory_space=pltpu.VMEM)


def params(mebibytes):
    return pltpu.CompilerParams(vmem_limit_bytes=mebibytes * 1024 * 1024)


def cost(flops, size):
    return pl.CostEstimate(flops=int(flops), bytes_accessed=int(size), transcendentals=0)


def edge_row(face, block, i, j):
    return jnp.broadcast_to(face[block, i, pl.ds(j, 1), :], (E, C))


def source_plane(x, top):
    return -1 if x == 0 else 1 if x == top + 1 else 0, top - 1 if x == 0 else 0 if x == top + 1 else x - 1


def block_at(neighbours, leaf, a, b, c):
    d = 9 * a + 3 * b + c
    if d == 0:
        return leaf
    n = neighbours[leaf, 13 + d if d < 0 else 12 + d]
    return jnp.where(n < 0, L, n & (L - 1))


def shifted_lines(table, lines, low, high, leaf, x, top, rows):
    a, i = source_plane(x, top)
    ends = (-1, 0, 1)
    at = [[block_at(table, leaf, a, b, c) if (c < 0 and low is not None) or c == 0 or (c > 0 and high is not None) else None for c in ends] for b in ends]
    ids = lax.broadcasted_iota(jnp.int32, (E, C), 0)
    out = ([], [], [])
    for y in rows:
        b = 0 if y == 0 else 2 if y == E + 1 else 1
        j = E - 1 if y == 0 else 0 if y == E + 1 else y - 1
        line = lines[at[b][1], i, E * j : E * j + E]
        below = jnp.where(ids == 0, 0.0 if low is None else edge_row(low, at[b][0], i, j), pltpu.roll(line, 1, 0))
        above = pltpu.roll(line, E - 1, 0)
        if high is not None:
            above = jnp.where(ids == E - 1, edge_row(high, at[b][2], i, j), above)
        for r, part in enumerate((below, line, above)):
            out[r].append(part)
    return out


def fill_plane(store, *where):
    parts = shifted_lines(*where, range(E + 2))
    whole = [jnp.concatenate(part, axis=0) for part in parts]
    for q in range(3):
        for r in range(3):
            store((3 * q + r) * C, whole[r][E * q : E * q + FACE].astype(bf16))


def banded(weight, first, second):
    zero = jnp.zeros((SPAN, C), bf16)
    w = [weight[9 * s : 9 * s + 9].reshape(SPAN, C) for s in range(3)]
    first[:SPAN, :C] = w[0]
    first[:SPAN, C:] = zero
    first[SPAN:, :C] = w[1]
    first[SPAN:, C:] = w[0]
    second[:SPAN, :C] = w[2]
    second[:SPAN, C:] = w[1]
    second[SPAN:, :C] = zero
    second[SPAN:, C:] = w[2]


def banded_turned(weight, first, second):
    zero = jnp.zeros((C, SPAN), bf16)
    w = [jnp.concatenate([weight[TAPS - 1 - t] for t in range(9 * s, 9 * s + 9)], axis=1) for s in range(3)]
    first[:C, :SPAN] = w[0]
    first[C:, :SPAN] = zero
    first[:C, SPAN:] = w[1]
    first[C:, SPAN:] = w[0]
    second[:C, :SPAN] = w[2]
    second[C:, :SPAN] = w[1]
    second[:C, SPAN:] = zero
    second[C:, SPAN:] = w[2]


def dot(x, w):
    return jnp.dot(x, w, preferred_element_type=f32)


def dot_turned(x, w):
    return lax.dot_general(x, w, (((1,), (1,)), ((), ())), preferred_element_type=f32)


def pairs_dot(multiply, cols, at, first, second):
    lo = cols[at : at + TOGETHER, 0:4].reshape(TOGETHER * 4 * FACE, 2 * SPAN)
    hi = cols[at : at + TOGETHER, 1:5].reshape(TOGETHER * 4 * FACE, 2 * SPAN)
    return multiply(lo, first[...]) + multiply(hi, second[...])


def half_planes(ref, leaf, half):
    return jnp.concatenate([ref[leaf, 2 * pair + half] for pair in range(4)], axis=0)


def spread_mask(voxels, leaf):
    return jnp.broadcast_to(voxels[leaf : leaf + 1, :].astype(f32), (C, E**3)).T


def faces_kernel(voxels, feat, cot, one, two, spread, held, coarse):
    for leaf in range(L):
        whole = spread_mask(voxels, leaf)
        spread[...] = whole
        coarse[...] = cot[leaf].astype(f32)
        edge = coarse[pl.ds(0, 16, stride=4), :]
        active = jnp.concatenate([spread[pl.ds(2 * FACE * i, 4, stride=16), :] for i in range(4)], axis=0)
        held[...] = feat[leaf].reshape(E**3, C).astype(f32) * whole
        up = held[pl.ds(E - 1, FACE, stride=E), :].astype(bf16)
        down = held[pl.ds(0, FACE, stride=E), :].astype(bf16)

        def write(below, above, leaf=leaf, up=up, down=down, edge=edge, active=active):
            out = (one, two)
            out[above][leaf, 0:FACE] = up
            out[above][leaf, FACE : FACE + 16] = jnp.zeros((16, C), bf16)
            out[below][leaf, 0:FACE] = down
            out[below][leaf, FACE : FACE + 16] = (edge * active).astype(bf16)

        by_parity(write)


def first_faces(voxels, feat, cot):
    return pl.pallas_call(
        faces_kernel,
        out_shape=(jax.ShapeDtypeStruct((L, FACE + 16, C), bf16),) * 2,
        in_specs=[vmem()] * 3,
        out_specs=(vmem(),) * 2,
        scratch_shapes=[pltpu.VMEM((E**3, C), f32), pltpu.VMEM((E**3, C), f32), pltpu.VMEM((64, C), f32)],
        compiler_params=params(12),
        cost_estimate=cost(6e9, 8e6),
        name="first_faces",
    )(voxels, feat, cot)


def setup_kernel(voxels, feat, cot, w1, w2, mask, lines, clines, active, upturned, wa, wb, wc, thin):
    lines[L] = jnp.zeros((E, FACE, C), f32)
    clines[L] = jnp.zeros((4, 4 * E, C), f32)
    thin[...] = jnp.zeros_like(thin)
    for leaf in range(L):
        whole = spread_mask(voxels, leaf)
        mask[leaf] = whole.reshape(E, FACE, C).astype(bf16)
        lines[leaf] = feat[leaf].astype(f32) * whole.reshape(E, FACE, C)
        starts = [2 * FACE * i + 2 * E * j for i in range(4) for j in range(4)]
        kept = jnp.concatenate([whole[at : at + E] for at in starts], axis=0)
        active[leaf] = kept.astype(bf16)
        thin[leaf, pl.ds(0, FACE, stride=2), :] = cot[leaf].astype(f32)
        upstream = thin[leaf] * kept
        clines[leaf] = upstream.reshape(4, 4 * E, C)
        upturned[:, 2 * FACE * leaf : 2 * FACE * leaf + 2 * FACE] = upstream.astype(bf16).T
    banded(w1, wa, wb)
    for n, p in enumerate((1, 2, 0)):
        for m, q in enumerate((1, 2, 0)):
            for r in range(3):
                at = (3 * m + r) * C
                wc[n * C : n * C + C, at : at + C] = w2[9 * p + 3 * q + 2 - r]


def setup(voxels, feat, cot, w1, w2):
    return pl.pallas_call(
        setup_kernel,
        out_shape=(
            jax.ShapeDtypeStruct((L, E, FACE, C), bf16),
            jax.ShapeDtypeStruct((L + 1, E, FACE, C), f32),
            jax.ShapeDtypeStruct((L + 1, 4, 4 * E, C), f32),
            jax.ShapeDtypeStruct((L, 2 * FACE, C), bf16),
            jax.ShapeDtypeStruct((C, L * 2 * FACE), bf16),
            jax.ShapeDtypeStruct((2 * SPAN, 2 * C), bf16),
            jax.ShapeDtypeStruct((2 * SPAN, 2 * C), bf16),
            jax.ShapeDtypeStruct((3 * C, SPAN), bf16),
        ),
        in_specs=[vmem()] * 5,
        out_specs=(vmem(),) * 8,
        scratch_shapes=[pltpu.VMEM((L, 2 * FACE, C), f32)],
        compiler_params=params(14),
        cost_estimate=cost(1e9, 8e6),
        name="setup",
    )(voxels, feat, cot, w1, w2)


def fill_coarse(store, table, clines, chigh, leaf, x):
    a, i = (1, 0) if x == 4 else (0, x)
    ids = lax.broadcasted_iota(jnp.int32, (E, C), 0)
    out = ([], [], [])
    for y in range(5):
        b, j = (1, 0) if y == 4 else (0, y)
        line = clines[block_at(table, leaf, a, b, 0), i, E * j : E * j + E]
        beyond = chigh[block_at(table, leaf, a, b, 1), 4 * i + j : 4 * i + j + 1, :]
        above = jnp.where(ids == E - 1, jnp.broadcast_to(beyond, (E, C)), pltpu.roll(line, E - 1, 0))
        for r, part in enumerate((pltpu.roll(line, 1, 0), line, above)):
            out[r].append(part)
    for r in range(3):
        whole = jnp.concatenate(out[r], axis=0)
        store(r * C, whole[: 4 * E].astype(bf16))
        store((3 + r) * C, whole[E:].astype(bf16))


def first_kernel(
    table, lines, clines, mask, one_in, two_in, wa, wb, wc,
    cols, hidden, delta, turned, one, two,
    low, high, chigh, ccols,
):
    low[L] = jnp.zeros((E, E, C), f32)
    high[L] = jnp.zeros((E, E, C), f32)
    chigh[L] = jnp.zeros((16, C), f32)
    hidden[L] = jnp.zeros((E, FACE, C), f32)
    delta[L] = jnp.zeros((E, FACE, C), f32)

    def receive(below, above):
        low_in, high_in = (one_in, two_in)[below], (one_in, two_in)[above]
        for leaf in range(L):
            low[leaf] = low_in[leaf, 0:FACE].astype(f32).reshape(E, E, C)
            high[leaf] = high_in[leaf, 0:FACE].astype(f32).reshape(E, E, C)
            chigh[leaf] = high_in[leaf, FACE : FACE + 16].astype(f32)

    by_parity(receive)

    def fill(n):
        for pair in range(5):
            for half in range(2):
                def store(at, value, pair=pair, half=half):
                    cols[n, pair, :, half * SPAN + at : half * SPAN + at + C] = value
                fill_plane(store, table, lines, low, high, n, 2 * pair + half, E)

            def store_coarse(at, value, pair=pair):
                ccols[n, pair, :, at : at + C] = value
            fill_coarse(store_coarse, table, clines, chigh, n, pair)

    for base in range(0, L, TOGETHER):
        for n in range(base, base + TOGETHER):
            fill(n)
        pre_all = pairs_dot(dot, cols, base, wa, wb)
        here = ccols[base : base + TOGETHER, 0:4].reshape(TOGETHER * 128, 6 * C)
        there = ccols[base : base + TOGETHER, 1:5].reshape(TOGETHER * 128, 6 * C)
        even, odd = slice(0, 3 * C), slice(3 * C, 9 * C)
        back = [dot_turned(here[:, : 3 * C], wc[: 2 * C, even]), dot_turned(here, wc[: 2 * C, odd])]
        back_next = [dot_turned(there[:, : 3 * C], wc[2 * C :, even]), dot_turned(there, wc[2 * C :, odd])]
        for n in range(base, base + TOGETHER):
            pre = pre_all[4 * FACE * (n - base) : 4 * FACE * (n - base) + 4 * FACE]
            sig = 1.0 / (1.0 + jnp.exp(-pre))
            slope = sig * (1.0 + pre * (1.0 - sig))
            for half in range(2):
                at = slice(half * C, half * C + C)
                m = half_planes(mask, n, half).astype(f32)
                h = m * pre[:, at] * sig[:, at]
                parts = [back[o][:, at] if half == 0 else back[o][:, at] + back_next[o] for o in range(2)]
                first_row = 128 * (n - base)
                rows = range(first_row, first_row + 128, E)
                g = jnp.concatenate([parts[o][i : i + E] for i in rows for o in range(2)], axis=0)
                d = g * m * slope[:, at]
                for pair in range(4):
                    rows = slice(FACE * pair, FACE * pair + FACE)
                    hidden[n, 2 * pair + half] = h[rows]
                    delta[n, 2 * pair + half] = d[rows]
                turned[half * C : half * C + C, 256 * n : 256 * n + 256] = d.astype(bf16).T

    def send(below, above):
        up, down = (one, two)[above], (one, two)[below]
        for n in range(L):
            for i in range(0, E, 2):
                def face(ref, k):
                    pair = [ref[n, i + m, pl.ds(k, E, stride=E), :] for m in range(2)]
                    return jnp.concatenate(pair, axis=0).astype(bf16)
                rows = slice(E * i, E * i + 2 * E)
                up[0, n, rows] = face(hidden, E - 1)
                up[1, n, rows] = face(delta, E - 1)
                down[0, n, rows] = face(delta, 0)
                down[1, n, rows] = jnp.zeros((2 * E, C), bf16)

    by_parity(send)


def first_conv(table, lines, clines, mask, faces, filters):
    return pl.pallas_call(
        first_kernel,
        out_shape=(
            jax.ShapeDtypeStruct((L, 5, FACE, 2 * SPAN), bf16),
            jax.ShapeDtypeStruct((L + 1, E, FACE, C), f32),
            jax.ShapeDtypeStruct((L + 1, E, FACE, C), f32),
            jax.ShapeDtypeStruct((2 * C, L * 256), bf16),
            jax.ShapeDtypeStruct((2, L, FACE, C), bf16),
            jax.ShapeDtypeStruct((2, L, FACE, C), bf16),
        ),
        in_specs=[smem()] + [vmem()] * 8,
        out_specs=(vmem(),) * 6,
        scratch_shapes=[
            pltpu.VMEM((L + 1, E, E, C), f32),
            pltpu.VMEM((L + 1, E, E, C), f32),
            pltpu.VMEM((L + 1, 16, C), f32),
            pltpu.VMEM((L, 5, 32, 6 * C), bf16),
        ],
        compiler_params=params(20),
        cost_estimate=cost(15e9, 18e6),
        name="first_conv",
    )(table, lines, clines, mask, *faces, *filters)


def split_halves(core, whole, kept, sent):
    mine = pl.multiple_of(core * HALF, HALF)
    theirs = pl.multiple_of(HALF - core * HALF, HALF)
    for t in range(TAPS):
        kept[t] = whole[t, pl.ds(mine, HALF), :]
        sent[t] = whole[t, pl.ds(theirs, HALF), :].astype(bf16)


def first_grad_kernel(cols, turned, kept, sent, total, whole):
    total[...] = jnp.zeros_like(total)
    for tile in range(9):
        lanes = range(256 * tile, 256 * tile + 256, C)
        for next_pair in range(2):
            rhs = cols[:, next_pair : next_pair + 4, :, 256 * tile : 256 * tile + 256].reshape(L * 4 * FACE, 256)
            for half in range(2):
                use = [lane for lane in lanes if 0 <= 2 * next_pair + lane // SPAN - half <= 2]
                if not use:
                    continue
                res = dot(turned[half * C : half * C + C, :], rhs)
                for lane in use:
                    p, o = 2 * next_pair + lane // SPAN - half, lane % SPAN
                    total[p, :, o : o + C] += res[:, lane - 256 * tile : lane - 256 * tile + C]

    for p in range(3):
        for t in range(9):
            whole[9 * p + t] = total[p, :, t * C : t * C + C].T
    split_halves(core_at(), whole, kept, sent)


def halves_shape():
    return jax.ShapeDtypeStruct((TAPS, HALF, C), f32), jax.ShapeDtypeStruct((TAPS, HALF, C), bf16)


def first_grad(cols, turned):
    return pl.pallas_call(
        first_grad_kernel,
        out_shape=halves_shape(),
        in_specs=[vmem(), vmem()],
        out_specs=(vmem(), vmem()),
        scratch_shapes=[
            pltpu.VMEM((3, C, SPAN), f32),
            pltpu.VMEM((TAPS, C, C), f32),
        ],
        compiler_params=params(16),
        cost_estimate=cost(6e9, 14e6),
        name="first_grad",
    )(cols, turned)


def second_kernel(
    table, lines, one_in, two_in, turned, sent_first,
    cols, kept, sent,
    low, total, whole,
):
    low[L] = jnp.zeros((E, E, C), f32)

    def receive(below, above):
        for leaf in range(L):
            low[leaf] = (one_in, two_in)[below][0, leaf].astype(f32).reshape(E, E, C)

    by_parity(receive)

    for leaf in range(L):
        for x in range(E + 1):
            parts = shifted_lines(table, lines, low, None, leaf, x, E, range(E + 1))
            for q in range(3):
                for r in range(3):
                    value = jnp.concatenate([parts[r][q + 2 * m] for m in range(4)], axis=0).astype(bf16)
                    at = (x % 2) * SPAN + (3 * q + r) * C
                    cols[leaf, x // 2, :, at : at + C] = value

    for tile in range(9):
        at = slice(256 * tile, 256 * tile + 256)
        total[:, at] = jnp.dot(turned[...], cols[:, 0:4, :, at].reshape(L * 2 * FACE, 256), preferred_element_type=f32)
    for tile in range(5):
        end = min(256 * tile + 256, SPAN)
        rhs = cols[:, 1:5, :, 256 * tile : end].reshape(L * 2 * FACE, end - 256 * tile)
        total[:, 2 * SPAN + 256 * tile : 2 * SPAN + end] = jnp.dot(turned[...], rhs, preferred_element_type=f32)
    for t in range(TAPS):
        whole[t] = total[:, t * C : t * C + C].T
    sent[0:TAPS] = sent_first[...]
    split_halves(core_at(), whole, kept, sent.at[TAPS:])


def second_grad(table, hidden, faces, upturned, sent_first):
    return pl.pallas_call(
        second_kernel,
        out_shape=(
            jax.ShapeDtypeStruct((L, 5, 32, 2 * SPAN), bf16),
            jax.ShapeDtypeStruct((TAPS, HALF, C), f32),
            jax.ShapeDtypeStruct((2 * TAPS, HALF, C), bf16),
        ),
        in_specs=[smem()] + [vmem()] * 5,
        out_specs=(vmem(),) * 3,
        scratch_shapes=[
            pltpu.VMEM((L + 1, E, E, C), f32),
            pltpu.VMEM((C, 3 * SPAN), f32),
            pltpu.VMEM((TAPS, C, C), f32),
        ],
        compiler_params=params(14),
        cost_estimate=cost(8e9, 6e6),
        name="second_grad",
    )(table, hidden, *faces, upturned, sent_first)


def coarse_kernel(cols, active, w2, coarse, thin):
    w = w2[...].reshape(TAPS * C, C)
    for leaf in range(L):
        lo = cols[leaf, 0:4].reshape(2 * FACE, 2 * SPAN)
        hi = cols[leaf, 1:5, :, 0:SPAN].reshape(2 * FACE, SPAN)
        thin[leaf] = (dot(lo, w[: 2 * SPAN]) + dot(hi, w[2 * SPAN :])) * active[leaf].astype(f32)
        coarse[leaf] = thin[leaf, pl.ds(0, FACE, stride=2), :].astype(bf16)


def coarse_conv(cols, active, w2):
    return pl.pallas_call(
        coarse_kernel,
        out_shape=jax.ShapeDtypeStruct((L, 64, C), bf16),
        in_specs=[vmem()] * 3,
        out_specs=vmem(),
        scratch_shapes=[pltpu.VMEM((L, 2 * FACE, C), f32)],
        compiler_params=params(12),
        cost_estimate=cost(1e9, 2e6),
        name="coarse_conv",
    )(cols, active, w2)


def adjoint_kernel(start, count, table, lines, mask, one_in, two_in, w, out, low, high, cols, wa, wb):
    low[L] = jnp.zeros((E, E, C), f32)
    high[L] = jnp.zeros((E, E, C), f32)

    def receive(below, above):
        for leaf in range(L):
            low[leaf] = (one_in, two_in)[below][1, leaf].astype(f32).reshape(E, E, C)
            high[leaf] = (one_in, two_in)[above][0, leaf].astype(f32).reshape(E, E, C)

    by_parity(receive)

    banded_turned(w, wa, wb)

    for base in range(0, count, TOGETHER):
        for n in range(base, base + TOGETHER):
            for pair in range(5):
                for half in range(2):
                    def store(at, value, n=n, pair=pair, half=half):
                        cols[n, pair, :, half * SPAN + at : half * SPAN + at + C] = value
                    fill_plane(store, table, lines, low, high, start + n, 2 * pair + half, E)
        res_all = pairs_dot(dot_turned, cols, base, wa, wb)
        for n in range(base, base + TOGETHER):
            res = res_all[4 * FACE * (n - base) : 4 * FACE * (n - base) + 4 * FACE]
            for half in range(2):
                m = half_planes(mask, start + n, half).astype(f32)
                value = (res[:, half * C : half * C + C] * m).astype(bf16)
                for pair in range(4):
                    out[n, 2 * pair + half] = value[FACE * pair : FACE * pair + FACE]


def adjoint_conv(start, count, table, delta, mask, faces, w):
    def kernel(*refs):
        adjoint_kernel(start, count, *refs)

    return pl.pallas_call(
        kernel,
        out_shape=jax.ShapeDtypeStruct((count, E, FACE, C), bf16),
        in_specs=[smem()] + [vmem()] * 5,
        out_specs=vmem(),
        scratch_shapes=[
            pltpu.VMEM((L + 1, E, E, C), f32),
            pltpu.VMEM((L + 1, E, E, C), f32),
            pltpu.VMEM((count, 5, FACE, 2 * SPAN), bf16),
            pltpu.VMEM((2 * C, 2 * SPAN), bf16),
            pltpu.VMEM((2 * C, 2 * SPAN), bf16),
        ],
        compiler_params=params(26),
        cost_estimate=cost(10e9 * count / L, 6e6),
        name="first_adjoint",
    )(table, delta, mask, *faces, w)


def start_sum_kernel(kept1, kept2, got, own, *sends):
    mine = ring_at()
    for d in range(4):
        rows = pl.ds(pl.multiple_of((mine ^ d) * PIECE, PIECE), PIECE)
        for t in range(2 * TAPS):
            kept, n = (kept1, t) if t < TAPS else (kept2, t - TAPS)
            value = kept[n, rows, :] + got[t, rows, :].astype(f32)
            if d == 0:
                own[t] = value
            else:
                sends[3 - d][t] = value.astype(bf16)


def start_sum(kept1, kept2, got):
    return pl.pallas_call(
        start_sum_kernel,
        out_shape=(jax.ShapeDtypeStruct((2 * TAPS, PIECE, C), f32),) + (jax.ShapeDtypeStruct((2 * TAPS, PIECE, C), bf16),) * 3,
        in_specs=[vmem()] * 3,
        out_specs=(vmem(),) * 4,
        compiler_params=params(12),
        cost_estimate=cost(1e6, 3e6),
        name="start_sum",
    )(kept1, kept2, got)


def next_sum_kernel(own, a, b, c, out):
    value = own[...] + a[...].astype(f32) + b[...].astype(f32) + c[...].astype(f32)
    out[0 : 2 * TAPS] = value.astype(bf16)
    out[2 * TAPS :] = jnp.zeros((out.shape[0] - 2 * TAPS, PIECE, C), bf16)


def next_sum(own, received, taps):
    return pl.pallas_call(
        next_sum_kernel,
        out_shape=jax.ShapeDtypeStruct((taps, PIECE, C), bf16),
        in_specs=[vmem()] * 4,
        out_specs=vmem(),
        compiler_params=params(8),
        cost_estimate=cost(1e6, 2e6),
        name="next_sum",
    )(own, *received)


def last_sum_kernel(factor, parts, out):
    total = parts[0].astype(f32)
    for n in range(1, parts.shape[0]):
        total = total + parts[n].astype(f32)
    total = (total * factor).astype(bf16)
    for n in range(parts.shape[0]):
        out[n] = total


def last_sum(parts, factor):
    def kernel(*refs):
        last_sum_kernel(factor, *refs)

    return pl.pallas_call(
        kernel,
        out_shape=jax.ShapeDtypeStruct(parts.shape, bf16),
        in_specs=[vmem()],
        out_specs=vmem(),
        compiler_params=params(8),
        cost_estimate=cost(1e6, 1e6),
        name="last_sum",
    )(parts)


def finish_kernel(*refs):
    mine, theirs, (first, second) = refs[0:4], refs[4:8], refs[8:10]
    at_y, at_x = lax.axis_index("scene") >> 1, lax.axis_index("leaf") & 3
    core = core_at()
    for parts, which in ((mine, core), (theirs, 1 - core)):
        at = jnp.where(which == 0, at_y, at_x)
        for d in range(4):
            row = pl.multiple_of(which * HALF + (at ^ d) * PIECE, PIECE)
            for t in range(2 * TAPS):
                out, n = (first, t) if t < TAPS else (second, t - TAPS)
                out[n, pl.ds(row, PIECE), :] = parts[d][t].astype(f32)


def finish(pieces):
    return pl.pallas_call(
        finish_kernel,
        out_shape=(jax.ShapeDtypeStruct((TAPS, C, C), f32),) * 2,
        in_specs=[vmem()] * 8,
        out_specs=(vmem(),) * 2,
        compiler_params=params(12),
        cost_estimate=cost(1e6, 6e6),
        name="finish",
    )(*pieces)


def ring_orders(leaf_count):
    out = []
    for d in range(1, 4):
        pairs = []
        for leaf in range(leaf_count):
            for scene in range(8):
                z, x, y, core = leaf // 4, leaf % 4, scene // 2, scene % 2
                x, y = (x, y ^ d) if core == 0 else (x ^ d, y)
                pairs.append((leaf * 8 + scene, (z * 4 + x) * 8 + y * 2 + core))
        out.append(pairs)
    return out


def rest_groups(leaf_count):
    depth = leaf_count // 4
    first = [[(z * 4 + x) * 8 + 2 * y for z in range(depth) for x in range(4)] for y in range(4)]
    second = [[(z * 4 + x) * 8 + 2 * y + 1 for z in range(depth) for y in range(4)] for x in range(4)]
    return first + second


def exchanged(first, second):
    count = lax.axis_size("leaf")
    pairs = [(i, i ^ 1) for i in range(count)]
    shifted = [(i, i + 1 if i % 2 else i - 1) for i in range(1, count - 1)]
    return lax.ppermute(first, "leaf", pairs), lax.ppermute(second, "leaf", shifted)


def to_other_core(block):
    return lax.ppermute(block, "scene", [(i, i ^ 1) for i in range(lax.axis_size("scene"))])


def shards(features, weight_first, weight_second, cotangent, neighbours, voxel_mask):
    both = ("leaf", "scene")
    leaf_count, scene_count = lax.axis_size("leaf"), lax.axis_size("scene")
    feat = features[0].reshape(L, E, FACE, C)
    cot = cotangent[0].reshape(L, 64, C)
    table = neighbours[0]
    voxels = voxel_mask[0]

    one, two = first_faces(voxels, feat, cot)
    with jax.named_scope("faces_in"):
        faces = exchanged(one, two)
    voxels, _ = lax.optimization_barrier((voxels, one))
    mask, lines, clines, active, upturned, *filters = setup(voxels, feat, cot, weight_first, weight_second)
    cols, hidden, delta, turned, one, two = first_conv(table, lines, clines, mask, faces, filters)
    with jax.named_scope("faces_mid"):
        faces = exchanged(one, two)
    kept1, sent1 = first_grad(cols, turned)
    cols2, kept2, sent = second_grad(table, hidden, faces, upturned, sent1)
    with jax.named_scope("sum_core"):
        got = to_other_core(sent)
    own, *sends = start_sum(kept1, kept2, got)
    orders, groups = ring_orders(leaf_count), rest_groups(leaf_count)
    per = -(-2 * TAPS // leaf_count)
    with jax.named_scope("sum_ring"):
        received = [lax.ppermute(s, both, o) for s, o in zip(sends, orders[::-1])]
    input_grad = adjoint_conv(0, L, table, delta, mask, faces, weight_first)
    own, input_grad = lax.optimization_barrier((own, input_grad))
    parts = next_sum(own, received, per * leaf_count).reshape(leaf_count, per * PIECE, C)
    with jax.named_scope("sum_rest"):
        parts = lax.all_to_all(parts, both, 0, 0, axis_index_groups=groups, tiled=True)
    parts = last_sum(parts, 1.0 / math.sqrt(leaf_count * scene_count * L * E**3))
    with jax.named_scope("gather_rest"):
        parts = lax.all_to_all(parts, both, 0, 0, axis_index_groups=groups, tiled=True)
    own = parts.reshape(per * leaf_count, PIECE, C)[: 2 * TAPS]
    with jax.named_scope("gather_ring"):
        received = [lax.ppermute(own, both, o) for o in orders]
    cols2, own = lax.optimization_barrier((cols2, own))
    coarse = coarse_conv(cols2, active, weight_second)
    coarse, late = lax.optimization_barrier((coarse, own))
    mine = [late] + [lax.optimization_barrier((piece, late))[0] for piece in received]
    with jax.named_scope("gather_core"):
        theirs = [to_other_core(piece) for piece in mine]
    grad_first, grad_second = finish([*mine, *theirs])
    return (
        coarse.reshape(1, L, 4, 4, 4, C),
        input_grad.reshape(1, L, E, E, E, C),
        grad_first,
        grad_second,
    )


def solution(mesh):
    placed = (
        P("scene", "leaf", None, None, None, None),
        P(),
        P(),
        P("scene", "leaf", None, None, None, None),
        P("scene", "leaf", None),
        P("scene", "leaf", None),
    )
    return jax.shard_map(
        shards,
        mesh=mesh,
        in_specs=placed,
        out_specs=(
            P("scene", "leaf", None, None, None, None),
            P("scene", "leaf", None, None, None, None),
            P(),
            P(),
        ),
        check_vma=False,
    )
```
